512 devices in a mesh: dp: 16 (over y, z_lo), tensor: 32 (over z_hi, x, core).
Axes of the slice: x: 4, y: 8, z: 8 (z_hi: 4, z_lo: 2; z = z_hi * 2 + z_lo), core: 2. Of those that a mesh axis runs over, the one named last changes fastest.
Arguments:
- tokens: bfloat16 [512, 8192], P('dp'), may hold values from -6 to 6
- gate_weight: bfloat16 [8192, 16384], P('dp', 'tensor'), may hold values from -0.0625 to 0.0625
- up_weight: bfloat16 [8192, 16384], P('dp', 'tensor'), may hold values from -0.0625 to 0.0625
- down_weight: bfloat16 [16384, 8192], P('tensor', 'dp'), may hold values from -6 to 6
- pruned_blocks: int32 [2], replicated, may hold values from 0 to 127, as said below
- panel_number: int32 [1], replicated, may hold values from 0 to 30
Outputs:
- factored_gram: float32 [16384, 16384], P('dp', 'tensor')
- compensation: float32 [16384, 8192], P('tensor', 'dp')
The draws below stay inside these ranges and needn't reach their ends.
Inputs may be any that keep to these rules, and one draw needn't show every extreme that they name: `pruned_blocks`: 2 distinct block numbers in any order, the last block of hidden units always among them; block b holds hidden units b * 128 to b * 128 + 127. `panel_number`: the panel holds hidden units 512 * p to 512 * p + 511 and some units follow it.
All inputs are finite; a program needn't handle non-finite values.
Results may differ from the reference program's by a relative error of at most 0.012.
The reference program's roundings to bfloat16 on the way (of `hidden`, `pruned_hidden` and `cross_gram`) count: a program that leaves them out, or rounds other values in their place, can miss the bound.
Values may be sent and summed in bfloat16 or wider, within the bound.
A program may use at most 64 MiB of HBM per device.

```python
import jax
import jax.numpy as jnp
from jax import lax

D = 8192
FW = 16384
PANEL = 512
BLOCK = 128
NPRUNE = 2
TOKENS = 512


def draw_pruned_blocks(key, part):
    key = jax.random.fold_in(key, 17)
    first_key, order_key = jax.random.split(key)
    others = jax.random.permutation(first_key, FW // BLOCK - 1)[:NPRUNE - 1]
    chosen = jnp.concatenate([others.astype(jnp.int32), jnp.full((1,), FW // BLOCK - 1, jnp.int32)])
    placing = jax.random.permutation(order_key, NPRUNE)
    return chosen[placing].astype(jnp.int32)


def block_levels(own_key, shape, pieces, low, largest):
    loudness = 1.0
    for axis_at, blocks in pieces:
        heights = jax.random.uniform(jax.random.fold_in(jax.random.fold_in(own_key, 6), axis_at), (blocks,), jnp.float32, low / len(pieces), largest / len(pieces))
        loudness = loudness * jnp.repeat(jnp.exp(heights), shape[axis_at] // blocks).reshape((-1,) + (1,) * (len(shape) - 1 - axis_at))
    return loudness


def normal_values(key, shape, width, reach, cuts=(), kind=jnp.bfloat16):
    factor_of = block_levels(key, shape, cuts, -0.22, 0.18) if cuts else 1.0
    result = jax.random.normal(key, shape, jnp.float32) * width * factor_of
    return jnp.minimum(jnp.maximum(result, -reach), reach).astype(kind)


def setup_inputs(seed: int = 0) -> dict:
    keys = jax.random.split(jax.random.key(seed), 7)
    return {
        "tokens": normal_values(keys[0], (TOKENS, D), 1.0, 6.0, ((0, 16),)),
        "gate_weight": normal_values(keys[1], (D, FW), D ** -0.5, 0.0625, ((0, 16), (1, 32))),
        "up_weight": normal_values(keys[2], (D, FW), D ** -0.5, 0.0625, ((0, 16), (1, 32))),
        "down_weight": normal_values(keys[3], (FW, D), 1.0, 6.0, ((0, 32), (1, 16))),
        "pruned_blocks": draw_pruned_blocks(jax.random.fold_in(keys[6], 71), 0),
        "panel_number": jax.random.randint(keys[5], (1,), 0, FW // PANEL - 1).astype(jnp.int32),
    }


DAMPING = 0.05
HIGHEST = lax.Precision.HIGHEST

def lower_solve(lower_factor, right_side):
    return lax.linalg.triangular_solve(lower_factor, right_side, left_side=True, lower=True)

def right_lower_solve(lower_factor, columns):
    return lax.linalg.triangular_solve(lower_factor, columns, left_side=False, lower=True, transpose_a=True)

def kept_flags(channel, pruned_blocks):
    return jnp.all((channel // BLOCK)[:, None] != pruned_blocks[None, :], axis=1)

def factor_rows(lower_factor, panel_columns, channel, panel_first):
    solved = right_lower_solve(lower_factor, panel_columns)
    return jnp.where((channel >= panel_first + PANEL)[:, None], solved, 0.0)

def reference(tokens, gate_weight, up_weight, down_weight, pruned_blocks, panel_number):
    gate_values = jnp.dot(tokens.astype(jnp.float32), gate_weight.astype(jnp.float32), preferred_element_type=jnp.float32)
    up_values = jnp.dot(tokens.astype(jnp.float32), up_weight.astype(jnp.float32), preferred_element_type=jnp.float32)
    hidden = (jax.nn.silu(gate_values) * up_values).astype(jnp.bfloat16)
    channel = jnp.arange(FW, dtype=jnp.int32)
    kept_mask = kept_flags(channel, pruned_blocks)
    raw_gram = jnp.dot(hidden.T.astype(jnp.float32), hidden.astype(jnp.float32), preferred_element_type=jnp.float32) / TOKENS
    kept_gram = jnp.where(kept_mask[:, None] & kept_mask[None, :], raw_gram, 0.0)
    kept_gram = kept_gram.at[channel, channel].add(jnp.where(kept_mask, DAMPING, 1.0))
    pruned_channel = (pruned_blocks[:, None] * BLOCK + jnp.arange(BLOCK, dtype=jnp.int32)[None, :]).reshape(-1)
    pruned_hidden = jnp.take(hidden, pruned_channel, axis=1)
    pruned_down = jnp.take(down_weight, pruned_channel, axis=0)
    cross_values = jnp.dot(hidden.T.astype(jnp.float32), pruned_hidden.astype(jnp.float32), preferred_element_type=jnp.float32) / TOKENS
    cross_gram = jnp.where(kept_mask[:, None], cross_values, 0.0).astype(jnp.bfloat16)
    right_side = jnp.dot(cross_gram.astype(jnp.float32), pruned_down.astype(jnp.float32), preferred_element_type=jnp.float32)
    panel_first = panel_number[0] * PANEL
    diag_panel = lax.dynamic_slice(kept_gram, (panel_first, panel_first), (PANEL, PANEL))
    lower_factor = jnp.linalg.cholesky(diag_panel)
    panel_columns = lax.dynamic_slice_in_dim(kept_gram, panel_first, PANEL, 1)
    factor = factor_rows(lower_factor, panel_columns, channel, panel_first)
    factored = kept_gram - jnp.dot(factor, factor.T, precision=HIGHEST)
    column_new = jnp.where((channel >= panel_first + PANEL)[:, None], factor, panel_columns)
    column_new = lax.dynamic_update_slice_in_dim(column_new, lower_factor, panel_first, 0)
    factored = lax.dynamic_update_slice_in_dim(factored, column_new, panel_first, 1)
    panel_right = lax.dynamic_slice_in_dim(right_side, panel_first, PANEL, 0)
    solved = lower_solve(lower_factor, panel_right)
    compensation = right_side - jnp.dot(factor, solved, precision=HIGHEST)
    compensation = lax.dynamic_update_slice_in_dim(compensation, solved, panel_first, 0)
    return (factored, compensation)
```

```python
import jax
import jax.numpy as jnp
from jax import lax
from jax.experimental import pallas as pl
from jax.experimental.pallas import tpu as pltpu
from jax.sharding import PartitionSpec as P

F32 = jnp.float32
BF16 = jnp.bfloat16
MESH = pl.DeviceIdType.MESH
DAMPING = 0.05
NDP = 16
NT = 32
NY = 8
WIDTH = 4

CHAINS = ((1, 0, 4), (-1, 1, 4), (1, 1, 3), (-1, 0, 3))


def split(x):
    hi = x.astype(BF16)
    return hi, (x - hi.astype(F32)).astype(BF16)


def dot(a, b, ca=1, cb=0):
    return lax.dot_general(a, b, (((ca,), (cb,)), ((), ())), preferred_element_type=F32)


def dot3(a, b, ca=1, cb=0):
    ah, al = split(a)
    bh, bl = split(b)
    return dot(ah, bh, ca, cb) + (dot(ah, bl, ca, cb) + dot(al, bh, ca, cb))


def drain(ref, sem):
    pltpu.make_async_copy(ref, ref, sem).wait()


def spread_kernel(
    tok, gate, up, down, pruned, panel,
    rowb, colb, pcb, pd,
    feat, pf, sb, rb, ssum, zr, hch, hpc, hold, obuf, gbuf, dbuf, dhold, dsel,
    s_tok, r_tok, s_sib, r_sib, s_ch, r_ch, s_z, r_z, s_d1, r_d1, s_d2, r_d2,
    s_p, r_p, s_pz, r_pz, s_ps, r_ps, s_row, r_row, s_col, r_col, s_e1, r_e1, s_e2, r_e2,
):
    i = lax.axis_index("dp")
    j = lax.axis_index("tensor")
    y, z = i // 2, i % 2
    zh, x, c = j // 8, (j // 2) % 4, j % 2
    sib = j + 1 - 2 * c
    other_z = i + 1 - 2 * z

    def remote(src, dst, send, recv, to):
        copy = pltpu.make_async_remote_copy(
            src_ref=src, dst_ref=dst, send_sem=send, recv_sem=recv, device_id=to, device_id_type=MESH
        )
        copy.start()
        return copy

    def here(src, dst, sem):
        pltpu.make_async_copy(src, dst, sem).start()

    def unless_self(same, src, dst, send, recv, to):
        @pl.when(same)
        def _():
            here(src, dst, recv)

        @pl.when(jnp.logical_not(same))
        def _():
            remote(src, dst, send, recv, to)

    barrier = pltpu.get_barrier_semaphore()

    def greet_dp(d, _):
        pl.semaphore_signal(barrier, inc=1, device_id=((i + d) % NDP, j), device_id_type=MESH)
        return 0

    def greet_t(d, _):
        pl.semaphore_signal(barrier, inc=1, device_id=(i, (j + d) % NT), device_id_type=MESH)
        return 0

    lax.fori_loop(1, NDP, greet_dp, 0)
    lax.fori_loop(1, NT, greet_t, 0)
    pl.semaphore_wait(barrier, NDP + NT - 2)

    def part(o):
        return tok.at[:, pl.ds(pl.multiple_of(512 * o + 256 * c, 256), 256)]

    mine = pl.ds(pl.multiple_of(32 * i, 32), 32)

    def send_tok(d, _):
        o = (i + d) % NDP
        remote(part(o), feat.at[c, mine, :], s_tok, r_tok, (o, j))
        return 0

    lax.fori_loop(1, NDP, send_tok, 0)
    here(part(i), feat.at[c, mine, :], r_tok)

    for n in range(2):
        quarter = pruned[n] % 4
        for e in range(8):
            rows = [down[128 * k + 16 * e : 128 * k + 16 * e + 16, :] for k in range(4)]
            low = jnp.where(quarter == 0, rows[0], rows[1])
            high = jnp.where(quarter == 2, rows[2], rows[3])
            dbuf[8 * n + e] = jnp.where(quarter < 2, low, high)

    def send_e1(e, _):
        to = 2 * e + e % 2
        unless_self(to == j, dbuf.at[e], dhold.at[j], s_e1, r_e1, (i, to))
        return 0

    lax.fori_loop(0, 16, send_e1, 0)
    is_down_holder = (j // 2) % 2 == c

    drain(feat.at[c], r_tok)
    remote(feat.at[c], feat.at[c], s_sib, r_sib, (i, sib))

    own = pl.ds(pl.multiple_of(256 * c, 256), 256)
    theirs = pl.ds(pl.multiple_of(256 * (1 - c), 256), 256)
    pf[:, :512] = dot(feat[c], gate[own, :])
    pf[:, 512:] = dot(feat[c], up[own, :])
    drain(feat.at[1 - c], r_sib)
    pf[:, :512] += dot(feat[1 - c], gate[theirs, :])
    pf[:, 512:] += dot(feat[1 - c], up[theirs, :])

    def value(yd, h):
        return pf[pl.ds(pl.multiple_of(64 * yd, 64), 64), 512 * h : 512 * h + 512]

    for s in range(1, 5):
        for n, (way, h, hops) in enumerate(CHAINS):
            if s > hops:
                continue
            v = value((y + way * (hops - s + 1) + NY) % NY, h)
            if s > 1:
                drain(rb.at[n, s - 2], r_ch.at[n, s - 2])
                v = v + rb[n, s - 2].astype(F32)
            sb[n, s - 1] = v.astype(BF16)
            to = 2 * ((y + way + NY) % NY) + z
            remote(sb.at[n, s - 1], rb.at[n, s - 1], s_ch.at[n, s - 1], r_ch.at[n, s - 1], (to, j))

    @pl.when(is_down_holder)
    def _():
        e = j // 2
        drain(dhold, r_e1)
        dsel[...] = jnp.where(e < 8, dhold[pruned[0] // 4], dhold[pruned[1] // 4])

        def send_e2(d, _):
            remote(dsel, pd.at[e], s_e2, r_e2, (i, (j + d) % NT))
            return 0

        lax.fori_loop(1, NT, send_e2, 0)
        here(dsel, pd.at[e], r_e2)

    for h in range(2):
        total = value(y, h)
        for n, (way, half, hops) in enumerate(CHAINS):
            if half == h:
                drain(rb.at[n, hops - 1], r_ch.at[n, hops - 1])
                total = total + rb[n, hops - 1].astype(F32)
        ssum[h] = total
        remote(
            ssum.at[h, pl.ds(pl.multiple_of(32 * (1 - z), 32), 32), :],
            zr.at[h], s_z.at[h], r_z.at[h], (other_z, j),
        )
    half_rows = pl.ds(pl.multiple_of(32 * z, 32), 32)
    drain(zr.at[0], r_z.at[0])
    g = ssum[0, half_rows, :] + zr[0]
    act = g / (1.0 + jnp.exp(-g))
    drain(zr.at[1], r_z.at[1])
    hidden = (act * (ssum[1, half_rows, :] + zr[1])).astype(BF16)
    for t in range(2):
        hch[t] = hidden[16 * t : 16 * t + 16, :]
        for q in range(4):
            hpc[4 * t + q] = hidden[16 * t : 16 * t + 16, 128 * q : 128 * q + 128]

    def send_d1(q, _):
        unless_self(4 * q == j, hpc.at[q], hold.at[j], s_d1, r_d1, (i, 4 * q))
        return 0

    lax.fori_loop(0, 8, send_d1, 0)

    def send_row(q, _):
        k = 8 * c + q
        ic = i // 8
        dst = rowb.at[ic, q % 4, 2 * c + q // 4, i % 8]
        same = (j // 2 == i) & (2 * k + ic == j)
        unless_self(same, hpc.at[q], dst, s_row.at[0], r_row.at[0], (j // 2, 2 * k + ic))
        return 0

    lax.fori_loop(0, 8, send_row, 0)

    @pl.when(j % 4 == 0)
    def _():
        drain(hold, r_d1)
        obuf[0] = hold[panel[0]]
        obuf[1] = hold[pruned[0] // 4]
        obuf[2] = hold[pruned[1] // 4]

        def send_d2(d, _):
            remote(obuf, gbuf.at[j // 4], s_d2, r_d2, (i, (j + d) % NT))
            return 0

        lax.fori_loop(1, NT, send_d2, 0)
        here(obuf, gbuf.at[j // 4], r_d2)

    drain(gbuf, r_d2)
    for q in range(4):
        pcb[c, y, z, :, 128 * q : 128 * q + 128] = gbuf[4 * c + q, 0]
    for n in range(2):
        pcb[c, y, z, :, 512 + 128 * n : 640 + 128 * n] = gbuf[4 * c + pruned[n] % 4, 1 + n]
    order = (1, 7, 2, 6, 3, 5, 4)
    for d in order:
        remote(
            pcb.at[c, y, z], pcb.at[c, y, z], s_p.at[d], r_p.at[d], (2 * ((y + d) % NY) + z, j)
        )
    remote(pcb.at[c, y, z], pcb.at[c, y, z], s_pz, r_pz, (other_z, j))
    for d in order:
        got = pcb.at[c, (y + NY - d) % NY, z]
        drain(got, r_p.at[d])
        remote(got, got, s_pz, r_pz, (other_z, j))
    remote(pcb.at[c, :, z], pcb.at[c, :, z], s_ps, r_ps, (i, sib))
    drain(pcb.at[c, :, 1 - z], r_pz)
    remote(pcb.at[c, :, 1 - z], pcb.at[c, :, 1 - z], s_ps, r_ps, (i, sib))

    def send_col(d, _):
        remote(hch, colb.at[:, i], s_col, r_col, ((i + d) % NDP, j))
        return 0

    lax.fori_loop(1, NDP, send_col, 0)
    here(hch, colb.at[:, i], r_col)

    part0 = rowb.at[c, x, zh]
    drain(part0, r_row.at[0])
    for d in range(1, 4):
        remote(part0, part0, s_row.at[1], r_row.at[1], (i, (j + 8 * d) % NT))
    drain(rowb.at[c, x, pl.ds(0, 3)], r_row.at[1])
    part1 = rowb.at[c, x]
    for d in range(1, 4):
        remote(part1, part1, s_row.at[2], r_row.at[2], (i, zh * 8 + ((x + d) % 4) * 2 + c))
    drain(rowb.at[c, pl.ds(0, 3)], r_row.at[2])
    remote(rowb.at[c], rowb.at[c], s_row.at[3], r_row.at[3], (i, sib))

    drain(pcb.at[1 - c], r_ps)
    drain(colb, r_col)
    drain(pd, r_e2)
    drain(rowb.at[1 - c], r_row.at[3])
    drain(feat.at[c, pl.ds(0, 480)], s_tok)
    drain(feat.at[c], s_sib)
    for n, (way, h, hops) in enumerate(CHAINS):
        for s in range(hops):
            drain(sb.at[n, s], s_ch.at[n, s])
    for h in range(2):
        drain(zr.at[h], s_z.at[h])

    @pl.when(j % 4 == 0)
    def _():
        drain(hpc.at[pl.ds(0, 7)], s_d1)

        def wait_d2(d, _):
            drain(obuf, s_d2)
            return 0

        lax.fori_loop(1, NT, wait_d2, 0)

    @pl.when(j % 4 != 0)
    def _():
        drain(hpc, s_d1)

    self_row = (j // 2 == i) & ((j // 2) // 8 == c) & (i // 8 == c)

    @pl.when(self_row)
    def _():
        drain(hpc.at[pl.ds(0, 7)], s_row.at[0])

    @pl.when(jnp.logical_not(self_row))
    def _():
        drain(hpc, s_row.at[0])

    @pl.when(is_down_holder)
    def _():
        drain(dbuf.at[pl.ds(0, 15)], s_e1)

        def wait_e2(d, _):
            drain(dsel, s_e2)
            return 0

        lax.fori_loop(1, NT, wait_e2, 0)

    @pl.when(jnp.logical_not(is_down_holder))
    def _():
        drain(dbuf, s_e1)

    for d in order:
        drain(pcb.at[c, y, z], s_p.at[d])
    drain(pcb.at[c, :, z], s_pz)
    drain(pcb.at[c], s_ps)
    drain(colb.at[:, pl.ds(0, 15)], s_col)
    drain(rowb.at[c, x, pl.ds(0, 3)], s_row.at[1])
    drain(rowb.at[c, pl.ds(0, 3)], s_row.at[2])
    drain(rowb.at[c], s_row.at[3])


def spread(tokens, gate, up, down, pruned, panel):
    vmem = pl.BlockSpec(memory_space=pltpu.VMEM)
    smem = pl.BlockSpec(memory_space=pltpu.SMEM)
    dma = pltpu.SemaphoreType.DMA
    return pl.pallas_call(
        spread_kernel,
        out_shape=(
            jax.ShapeDtypeStruct((2, 4, 4, 8, 16, 128), BF16),
            jax.ShapeDtypeStruct((2, 16, 16, 512), BF16),
            jax.ShapeDtypeStruct((2, 8, 2, 16, 768), BF16),
            jax.ShapeDtypeStruct((16, 16, 512), BF16),
        ),
        in_specs=[vmem] * 4 + [smem] * 2,
        out_specs=(vmem,) * 4,
        scratch_shapes=[
            pltpu.VMEM((2, 512, 256), BF16),
            pltpu.VMEM((512, 1024), F32),
            pltpu.VMEM((4, 4, 64, 512), BF16),
            pltpu.VMEM((4, 4, 64, 512), BF16),
            pltpu.VMEM((2, 64, 512), F32),
            pltpu.VMEM((2, 32, 512), F32),
            pltpu.VMEM((2, 16, 512), BF16),
            pltpu.VMEM((8, 16, 128), BF16),
            pltpu.VMEM((32, 16, 128), BF16),
            pltpu.VMEM((3, 16, 128), BF16),
            pltpu.VMEM((8, 3, 16, 128), BF16),
            pltpu.VMEM((16, 16, 512), BF16),
            pltpu.VMEM((32, 16, 512), BF16),
            pltpu.VMEM((16, 512), BF16),
            dma, dma, dma, dma, dma((4, 4)), dma((4, 4)), dma((2,)), dma((2,)), dma, dma, dma, dma,
            dma((8,)), dma((8,)), dma, dma, dma, dma, dma((4,)), dma((4,)), dma, dma, dma, dma, dma, dma,
        ],
        compiler_params=pltpu.CompilerParams(
            collective_id=0, has_side_effects=True, vmem_limit_bytes=48 << 20
        ),
        name="spread",
    )(tokens, gate, up, down, pruned, panel)


def small_factor(p, w):
    low = [[None] * w for _ in range(w)]
    inv = [[None] * w for _ in range(w)]
    a = {(r, c): p[r][c] for r in range(w) for c in range(r + 1)}
    for c in range(w):
        s = lax.rsqrt(a[c, c])
        inv[c][c] = s
        for r in range(c + 1, w):
            low[r][c] = a[r, c] * s
        for r in range(c + 1, w):
            for q in range(c + 1, r + 1):
                a[r, q] = a[r, q] - low[r][c] * low[q][c]
    for r in range(w):
        for c in range(r):
            t = sum(low[r][k] * inv[k][c] for k in range(c, r))
            inv[r][c] = -(t * inv[r][r])
    return inv


def eliminate(t, w, n=128):
    lane = lax.broadcasted_iota(jnp.int32, (1, n), 1)
    m_rows, u_rows = [], []
    for k in range(0, n, w):
        base = n - t.shape[0]
        cols = [jnp.broadcast_to(t[:, k + q : k + q + 1], t.shape) for q in range(w)]
        p = [[cols[q][k + r - base : k + r - base + 1, :] for q in range(r + 1)] for r in range(w)]
        inv = small_factor(p, w)
        rows = [t[k + q - base : k + q - base + 1, :] for q in range(w)]
        inside = (lane >= k) & (lane < k + w)
        ident = [jnp.where(inside, (lane == k + q).astype(F32), rows[q]) for q in range(w)]
        for r in range(w):
            comb = sum(inv[r][q] * rows[q] for q in range(r + 1))
            m = jnp.where(lane < k, comb, 0.0)
            for q in range(r + 1):
                m = jnp.where(lane == k + q, inv[r][q], m)
            m_rows.append(m)
            u_rows.append(jnp.where(lane >= k + r, comb, 0.0))
        if k + w == n:
            break
        nb = ((k + w) // 8) * 8
        t = t[nb - base :, :]
        cols = [col[nb - base :, :] for col in cols]
        f = [sum(cols[q] * inv[r][q] for q in range(r + 1)) for r in range(w)]
        mult = [sum(f[r] * inv[r][q] for r in range(q, w)) for q in range(w)]
        t = jnp.where(inside, 0.0, t)
        for q in range(w):
            t = t - mult[q] * ident[q]
    return jnp.concatenate(m_rows, 0), jnp.concatenate(u_rows, 0)


def factor_panel(t_ref, m_ref, u_ref):
    zeros = jnp.zeros((128, 128), F32)
    for b in range(4):
        s0 = 128 * b
        m, u = eliminate(t_ref[s0 : s0 + 128, s0 : s0 + 128], WIDTH)
        s = dot3(m, t_ref[s0 : s0 + 128, :])
        parts = [s[:, 128 * q : 128 * q + 128] for q in range(4)]
        parts[b] = m
        for q in range(4):
            lanes = slice(128 * q, 128 * q + 128)
            m_ref[s0 : s0 + 128, lanes] = parts[q] if q <= b else zeros
            u_ref[s0 : s0 + 128, lanes] = parts[q] if q > b else (u if q == b else zeros)
        if b < 3:
            s = jnp.concatenate(parts, 1)
            rest = s0 + 128
            update = dot3(jnp.transpose(s[:, rest:]), s)
            for q in range(4):
                lanes = slice(128 * q, 128 * q + 128)
                old = t_ref[rest:, lanes] if q != b else 0.0
                t_ref[rest:, lanes] = old - update[:, lanes]


def finish_kernel(rowb, colb, pcb, pd, pruned, panel, fout, cout, t_ref, m_ref, u_ref):
    i = lax.axis_index("dp")
    j = lax.axis_index("tensor")
    p = panel[0]
    b0, b1 = pruned[0], pruned[1]
    lane = lax.broadcasted_iota(jnp.int32, (1, 512), 1)

    def kept(block512):
        blk = block512 * 4 + lane // 128
        return (blk != b0) & (blk != b1)

    def damping(keep):
        r = lax.broadcasted_iota(jnp.int32, (512, 512), 0)
        q = lax.broadcasted_iota(jnp.int32, (512, 512), 1)
        return jnp.where(r == q, jnp.where(keep, DAMPING, 1.0), 0.0)

    scale = 1.0 / 512
    p_kept = kept(p)
    c_kept = kept(j)
    hp = jnp.where(p_kept, pcb[:, :, :, :, :512].reshape(512, 512), 0.0).astype(BF16)
    hpr = pcb[:, :, :, :, 512:].reshape(512, 256)
    hc = jnp.where(c_kept, colb[...].reshape(512, 512), 0.0).astype(BF16)
    hpt = jnp.transpose(hp)
    hct = jnp.transpose(hc)
    t_ref[...] = dot(hpt, hp) * scale + damping(p_kept)
    kc = dot(hct, hp) * scale
    cross_c = (dot(hct, hpr) * scale).astype(BF16)
    cross_p = (dot(hpt, hpr) * scale).astype(BF16)

    factor_panel(t_ref, m_ref, u_ref)
    m = m_ref[...]
    below = (j > p).astype(F32)
    inside = (j == p).astype(F32)
    r = lax.broadcasted_iota(jnp.int32, (512, 512), 0)
    q = lax.broadcasted_iota(jnp.int32, (512, 512), 1)
    fc = dot3(kc, m, 1, 1) * below - jnp.where(r == q, inside, 0.0)
    gh, gl = split(dot3(fc, m))
    outside = 1.0 - inside
    rest = hc.astype(F32) * outside - (dot(hp, gh, 1, 1) + dot(hp, gl, 1, 1))
    zh, zl = split(cross_c.astype(F32) * outside - (dot(gh, cross_p) + dot(gl, cross_p)))
    down = pd[...].reshape(256, 512)
    cout[...] = dot(zh, down) + dot(zl, down)
    for h in range(2):
        row = 2 * i + h
        r_kept = kept(row)
        hr = jnp.concatenate(
            [
                jnp.concatenate(
                    [rowb[ic, cc, 2 * h + t].reshape(128, 128) for t in range(2) for ic in range(2)], 0
                )
                for cc in range(4)
            ],
            1,
        )
        hrt = jnp.transpose(jnp.where(r_kept, hr, 0.0).astype(BF16))
        rows = slice(512 * h, 512 * h + 512)

        @pl.when(row > p)
        def _():
            rh, rl = split(rest)
            fout[rows, :] = (dot(hrt, rh) + dot(hrt, rl)) * scale

        @pl.when(row <= p)
        def _():
            fout[rows, :] = dot(hrt, hc) * scale

        @pl.when(row == j)
        def _():
            fout[rows, :] += damping(r_kept)

        @pl.when((row == p) & (j == p))
        def _():
            fout[rows, :] = jnp.transpose(u_ref[...])


def finish(rowb, colb, pcb, pd, pruned, panel):
    vmem = pl.BlockSpec(memory_space=pltpu.VMEM)
    smem = pl.BlockSpec(memory_space=pltpu.SMEM)
    return pl.pallas_call(
        finish_kernel,
        out_shape=(jax.ShapeDtypeStruct((1024, 512), F32), jax.ShapeDtypeStruct((512, 512), F32)),
        in_specs=[vmem] * 4 + [smem] * 2,
        out_specs=(vmem,) * 2,
        scratch_shapes=[pltpu.VMEM((512, 512), F32)] * 3,
        compiler_params=pltpu.CompilerParams(vmem_limit_bytes=56 << 20),
        name="finish",
    )(rowb, colb, pcb, pd, pruned, panel)


def local(tokens, gate_weight, up_weight, down_weight, pruned_blocks, panel_number):
    spread_out = spread(tokens, gate_weight, up_weight, down_weight, pruned_blocks, panel_number)
    return finish(*spread_out, pruned_blocks, panel_number)


def solution(mesh):
    in_specs = (P("dp", None), P("dp", "tensor"), P("dp", "tensor"), P("tensor", "dp"), P(), P())
    out_specs = (P("dp", "tensor"), P("tensor", "dp"))
    return jax.shard_map(local, mesh=mesh, in_specs=in_specs, out_specs=out_specs, check_vma=False)
```

```python
import jax
import jax.numpy as jnp
from jax import lax
from jax.experimental import pallas as pl
from jax.experimental.pallas import tpu as pltpu
from jax.sharding import PartitionSpec as P

F32 = jnp.float32
BF16 = jnp.bfloat16
MESH = pl.DeviceIdType.MESH
DAMPING = 0.05
NDP = 16
NT = 32
NY = 8
WIDTH = 8

LONG = ((1, 0, 4), (-1, 2, 4), (1, 1, 4), (-1, 3, 4))
SHORT = ((1, 2, 3), (-1, 0, 3), (1, 3, 3), (-1, 1, 3))
CHAINS = LONG + SHORT


def split(x):
    hi = x.astype(BF16)
    return hi, (x - hi.astype(F32)).astype(BF16)


def dot(a, b, ca=1, cb=0):
    return lax.dot_general(a, b, (((ca,), (cb,)), ((), ())), preferred_element_type=F32)


def dot3(a, b, ca=1, cb=0):
    ah, al = split(a)
    bh, bl = split(b)
    return dot(ah, bh, ca, cb) + (dot(ah, bl, ca, cb) + dot(al, bh, ca, cb))


def eliminate(t, w, n=128):
    lane = lax.broadcasted_iota(jnp.int32, (1, n), 1)
    nb = w // 2
    m_rows, u_rows = [], []
    for k in range(0, n, w):
        base = n - t.shape[0]
        cols = [jnp.broadcast_to(t[:, k + q : k + q + 1], t.shape) for q in range(w)]
        a = {(r, q): cols[q][k + r - base : k + r - base + 1, :] for r in range(w) for q in range(r + 1)}
        rows = [t[k + q - base : k + q - base + 1, :] for q in range(w)]
        inside = (lane >= k) & (lane < k + w)
        ident = [jnp.where(inside, (lane == k + q).astype(F32), rows[q]) for q in range(w)]
        nxt = (k + w) // 8 * 8
        if k + w < n:
            cols = [col[nxt - base :, :] for col in cols]
            new = jnp.where(inside, 0.0, t[nxt - base :, :])
        for b in range(nb):
            i0, i1 = 2 * b, 2 * b + 1
            p, q, s = a[i0, i0], a[i1, i0], a[i1, i1]
            d = 1.0 / (p * s - q * q)
            ia, ib, ic = s * d, -(q * d), p * d
            r0 = lax.rsqrt(p)
            l = q * r0
            r1 = lax.rsqrt(s - l * l)
            for src, out, keep in ((ident, m_rows, lane < k + w), (rows, u_rows, None)):
                x0 = src[i0] * r0
                x1 = (src[i1] - x0 * l) * r1
                if keep is None:
                    out += [jnp.where(lane >= k + i0, x0, 0.0), jnp.where(lane >= k + i1, x1, 0.0)]
                else:
                    out += [jnp.where(keep, x0, 0.0), jnp.where(keep, x1, 0.0)]
            for r in range(i1 + 1, w):
                f0 = a[r, i0] * ia + a[r, i1] * ib
                f1 = a[r, i0] * ib + a[r, i1] * ic
                for c in range(i1 + 1, r + 1):
                    a[r, c] = a[r, c] - (f0 * a[c, i0] + f1 * a[c, i1])
                if k + w < n:
                    cols[r] = cols[r] - (cols[i0] * f0 + cols[i1] * f1)
                ident[r] = ident[r] - (f0 * ident[i0] + f1 * ident[i1])
                rows[r] = rows[r] - (f0 * rows[i0] + f1 * rows[i1])
            if k + w < n:
                g0 = ident[i0] * ia + ident[i1] * ib
                g1 = ident[i0] * ib + ident[i1] * ic
                new = new - (cols[i0] * g0 + cols[i1] * g1)
        if k + w < n:
            t = new
    return jnp.concatenate(m_rows, 0), jnp.concatenate(u_rows, 0)


def drain(ref, sem):
    pltpu.make_async_copy(ref, ref, sem).wait()


def body(
    tok_in, gate_in, up_in, down_in, pruned, panel,
    fout, cout,
    tok, gate, up, down, feat, pf, sb, rb, rl, zs_own, zr, hch, hpc, xb, zs, zr2, zb, zb2, pcb,
    colb, rowb, dx, dxr, dz, dzr, pd, t_ref, s_ref, m_ref, u_ref,
    s_in, hello, s_tok, r_tok, s_sib, r_sib, s_ch, r_ch, s_last, r_last, s_z, r_z,
    s_x, r_x, s_zh, r_zh, s_p, r_p, s_ps, r_ps, s_row, r_row, s_col, r_col, s_d, r_d,
):
    i = lax.axis_index("dp")
    j = lax.axis_index("tensor")
    y, z = i // 2, i % 2
    zh, x, c = j // 8, (j // 2) % 4, j % 2
    e8 = j % 8
    sib = j + 1 - 2 * c
    other_z = i + 1 - 2 * z

    def remote(src, dst, send, recv, to):
        pltpu.make_async_remote_copy(
            src_ref=src, dst_ref=dst, send_sem=send, recv_sem=recv, device_id=to, device_id_type=MESH
        ).start()

    def here(src, dst, sem):
        pltpu.make_async_copy(src, dst, sem).start()

    def signal(sem, to):
        pl.semaphore_signal(sem, inc=1, device_id=to, device_id_type=MESH)

    def line(d):
        return j - e8 + (e8 + d) % 8

    for n, (src, dst) in enumerate(((tok_in, tok), (gate_in, gate), (up_in, up), (down_in, down))):
        here(src, dst, s_in.at[n])

    barrier = pltpu.get_barrier_semaphore()

    def greet_dp(d, _):
        signal(barrier, ((i + d) % NDP, j))
        return 0

    def greet_line(d, _):
        signal(barrier, (i, line(d)))
        return 0

    def greet_zh(d, _):
        signal(barrier, (i, (j + 8 * d) % NT))
        return 0

    lax.fori_loop(1, NDP, greet_dp, 0)
    lax.fori_loop(1, 4, greet_zh, 0)
    lax.fori_loop(1, 8, greet_line, 0)
    drain(tok, s_in.at[0])
    pl.semaphore_wait(barrier, NDP - 1 + 3 + 7)

    def send_tok(o, g):
        src = tok.at[:, pl.ds(pl.multiple_of(512 * o + 256 * c, 256), 256)]
        dst = feat.at[c, y, pl.ds(pl.multiple_of(32 * z, 32), 32), :]
        remote(src, dst, s_tok, r_tok.at[g], (o, j))

    for g in (4, 3, 2, 1, 0):
        for way in (1, -1) if g in (1, 2, 3) else (1,):
            yo = (y + way * g + NY) % NY
            for zo in (z, 1 - z):
                if g == 0 and zo is z:
                    src = tok.at[:, pl.ds(pl.multiple_of(512 * i + 256 * c, 256), 256)]
                    here(src, feat.at[c, y, pl.ds(pl.multiple_of(32 * z, 32), 32), :], r_tok.at[0])
                else:
                    send_tok(2 * yo + zo, g)
    for d in range(1, 4):
        signal(hello, (i, (j + 8 * d) % NT))

    drain(down, s_in.at[3])
    for n in range(2):
        quarter = pruned[n] % 4
        for e in range(8):
            rows = [down[128 * k + 16 * e : 128 * k + 16 * e + 16, :] for k in range(4)]
            low = jnp.where(quarter == 0, rows[0], rows[1])
            high = jnp.where(quarter == 2, rows[2], rows[3])
            dx[e, n] = jnp.where(quarter < 2, low, high)

    def send_dx(d, _):
        e = (e8 + d) % 8
        remote(dx.at[e], dxr.at[e8], s_d.at[0], r_d.at[0], (i, line(d)))
        return 0

    lax.fori_loop(1, 8, send_dx, 0)
    here(dx.at[e8], dxr.at[e8], r_d.at[0])

    def blocks(g):
        return ((y + g) % NY, (y + NY - g) % NY) if g in (1, 2, 3) else ((y + g) % NY,)

    def forward(g):
        drain(feat.at[c, pl.ds(0, len(blocks(g)))], r_tok.at[g])
        for yb in blocks(g):
            remote(feat.at[c, yb], feat.at[c, yb], s_sib, r_sib.at[g], (i, sib))

    drain(gate, s_in.at[1])
    drain(up, s_in.at[2])

    def multiply(g):
        bs = blocks(g)
        drain(feat.at[c, pl.ds(0, len(bs))], r_sib.at[g])
        halves = [jnp.concatenate([feat[k, yb] for yb in bs], 0) for k in range(2)]
        for h, w in enumerate((gate, up)):
            v = dot(halves[0], w[:256, :]) + dot(halves[1], w[256:, :])
            for k, yb in enumerate(bs):
                pf[yb, :, 512 * h : 512 * h + 512] = v[64 * k : 64 * k + 64]

    def chain(n, s):
        way, h, hops = CHAINS[n]
        yd = (y + way * (hops - s + 1) + NY) % NY
        v = pf[yd, :, 256 * h : 256 * h + 256]
        if s > 1:
            drain(rb.at[n, s - 2], r_ch.at[n, s - 2])
            v = v + rb[n, s - 2].astype(F32)
        sb[n, s - 1] = v.astype(BF16)
        to = 2 * ((y + way + NY) % NY)
        if s < hops:
            remote(sb.at[n, s - 1], rb.at[n, s - 1], s_ch.at[n, s - 1], r_ch.at[n, s - 1], (to + z, j))
        else:
            for zo in (z, 1 - z):
                part = sb.at[n, s - 1, pl.ds(pl.multiple_of(32 * zo, 32), 32), :]
                remote(part, rl.at[n, z], s_last.at[n], r_last.at[n], (to + zo, j))

    def long(s):
        for n in range(4):
            chain(n, s)

    def short(s):
        for n in range(4, 8):
            chain(n, s)

    pl.semaphore_wait(hello, 3)
    forward(4)
    forward(3)
    multiply(4)
    long(1)
    forward(2)
    multiply(3)
    short(1)
    forward(1)
    multiply(2)
    long(2)
    drain(dxr, r_d.at[0])
    for n in range(2):
        dz[n] = dxr[(pruned[n] // 4) % 8, n]
    for d in range(1, 4):
        remote(dz, dzr.at[zh], s_d.at[1], r_d.at[1], (i, (j + 8 * d) % NT))
    here(dz, dzr.at[zh], r_d.at[1])
    short(2)
    forward(0)
    multiply(1)
    long(3)
    multiply(0)
    own_rows = pl.ds(pl.multiple_of(32 * z, 32), 32)
    zs_own[...] = pf[y, pl.ds(pl.multiple_of(32 * (1 - z), 32), 32), :].astype(BF16)
    remote(zs_own, zr, s_z, r_z, (other_z, j))
    short(3)
    long(4)
    drain(dzr, r_d.at[1])
    for n in range(2):
        pd[n, e8] = dzr[pruned[n] // 32, n]

    def send_pd(d, _):
        remote(pd.at[:, e8], pd.at[:, e8], s_d.at[2], r_d.at[2], (i, line(d)))
        return 0

    lax.fori_loop(1, 8, send_pd, 0)

    drain(zr, r_z)
    total = []
    for h in range(2):
        quarters = []
        for k in (2 * h, 2 * h + 1):
            v = pf[y, own_rows, 256 * k : 256 * k + 256] + zr[:, 256 * k : 256 * k + 256].astype(F32)
            for n in (4, 5, 6, 7, 0, 1, 2, 3):
                if CHAINS[n][1] == k:
                    drain(rl.at[n], r_last.at[n])
                    v = v + (rl[n, 0].astype(F32) + rl[n, 1].astype(F32))
            quarters.append(v)
        total.append(jnp.concatenate(quarters, 1))
    g, u = total
    hidden = (g / (1.0 + jnp.exp(-g)) * u).astype(BF16)
    for t in range(2):
        hch[t] = hidden[16 * t : 16 * t + 16, :]

    def send_x(d, _):
        e = (e8 + d) % 8
        remote(hch.at[e % 2], xb.at[e8], s_x, r_x, (i, line(d)))
        return 0

    lax.fori_loop(1, 8, send_x, 0)
    here(hch.at[c], xb.at[e8], r_x)

    for t in range(2):
        for q in range(4):
            hpc[4 * t + q] = hidden[16 * t : 16 * t + 16, 128 * q : 128 * q + 128]

    def send_row(q, _):
        k = 8 * c + q
        ic = i // 8
        dst = rowb.at[ic, q % 4, 2 * c + q // 4, i % 8]
        same = (j // 2 == i) & (2 * k + ic == j)

        @pl.when(same)
        def _():
            here(hpc.at[q], dst, r_row.at[0])

        @pl.when(jnp.logical_not(same))
        def _():
            remote(hpc.at[q], dst, s_row.at[0], r_row.at[0], (j // 2, 2 * k + ic))

        return 0

    lax.fori_loop(0, 8, send_row, 0)

    drain(xb, r_x)
    chosen = xb[panel[0] % 8]
    for q in range(4):
        zs[q] = chosen[:, 128 * q : 128 * q + 128]
    for d in range(1, 4):
        remote(zs, zb.at[zh], s_zh.at[0], r_zh.at[0], (i, (j + 8 * d) % NT))
    here(zs, zb.at[zh], r_zh.at[0])
    for n in range(2):
        quarter = pruned[n] % 4
        rows = [xb[(pruned[n] // 4) % 8, :, 128 * k : 128 * k + 128] for k in range(4)]
        low = jnp.where(quarter == 0, rows[0], rows[1])
        high = jnp.where(quarter == 2, rows[2], rows[3])
        zr2[n] = jnp.where(quarter < 2, low, high)
    for d in range(1, 4):
        remote(zr2, zb2.at[zh], s_zh.at[1], r_zh.at[1], (i, (j + 8 * d) % NT))
    here(zr2, zb2.at[zh], r_zh.at[1])

    def send_dp(part, n):
        def one(d, _):
            remote(part, part, s_p.at[n], r_p.at[n], ((i + d) % NDP, j))
            return 0

        lax.fori_loop(1, NDP, one, 0)

    def panel_part(n):
        return (pl.ds(0, 1), pl.ds(1, 3), pl.ds(4, 2))[n]

    drain(zb, r_zh.at[0])
    for q in range(4):
        pcb[c, i, q] = zb[panel[0] // 8, q]
    send_dp(pcb.at[c, i, panel_part(0)], 0)
    send_dp(pcb.at[c, i, panel_part(1)], 1)
    drain(zb2, r_zh.at[1])
    for n in range(2):
        pcb[c, i, 4 + n] = zb2[pruned[n] // 32, n]
    send_dp(pcb.at[c, i, panel_part(2)], 2)

    def send_col(d, _):
        remote(hch, colb.at[:, y, z], s_col.at[0], r_col.at[0], (2 * ((y + d) % NY) + z, j))
        return 0

    lax.fori_loop(1, NY, send_col, 0)
    here(hch, colb.at[:, y, z], r_col.at[0])

    def columns_over_z():
        same_z = colb.at[:, :, z]
        drain(same_z, r_col.at[0])
        remote(same_z, same_z, s_col.at[1], r_col.at[1], (other_z, j))

    def to_sibling(n):
        part = panel_part(n)
        drain(pcb.at[c, pl.ds(0, 15), part], r_p.at[n])
        remote(pcb.at[c, :, part], pcb.at[c, :, part], s_ps.at[n], r_ps.at[n], (i, sib))

    def from_sibling(n):
        drain(pcb.at[1 - c, :, panel_part(n)], r_ps.at[n])

    part0 = rowb.at[c, x, zh]
    part1 = rowb.at[c, x]
    part2 = rowb.at[c]

    def rows_over_z():
        drain(part0, r_row.at[0])
        for d in range(1, 4):
            remote(part0, part0, s_row.at[1], r_row.at[1], (i, (j + 8 * d) % NT))

    def rows_over_x():
        drain(rowb.at[c, x, pl.ds(0, 3)], r_row.at[1])
        for d in range(1, 4):
            remote(part1, part1, s_row.at[2], r_row.at[2], (i, zh * 8 + ((x + d) % 4) * 2 + c))

    def rows_over_cores():
        drain(rowb.at[c, pl.ds(0, 3)], r_row.at[2])
        remote(part2, part2, s_row.at[3], r_row.at[3], (i, sib))

    rows_over_z()
    to_sibling(0)

    lane = lax.broadcasted_iota(jnp.int32, (1, 512), 1)
    scale = 1.0 / 512
    b0, b1 = pruned[0], pruned[1]
    p = panel[0]

    def kept(block512):
        blk = block512 * 4 + lane // 128
        return (blk != b0) & (blk != b1)

    def damping(keep):
        n = keep.shape[1]
        r = lax.broadcasted_iota(jnp.int32, (n, n), 0)
        q = lax.broadcasted_iota(jnp.int32, (n, n), 1)
        return jnp.where(r == q, jnp.where(keep, DAMPING, 1.0), 0.0)

    p_kept = kept(p)
    from_sibling(0)
    hp0 = jnp.where(p_kept[:, :128], pcb[:, :, 0].reshape(512, 128), 0.0).astype(BF16)
    t_ref[:128, :128] = dot(jnp.transpose(hp0), hp0) * scale + damping(p_kept[:, :128])

    def factor_block(b, _):
        s0 = pl.multiple_of(128 * b, 128)
        at = pl.ds(s0, 128)
        m, u = eliminate(t_ref[at, at], WIDTH)

        @pl.when(b == 0)
        def _():
            to_sibling(1)
            from_sibling(1)
            hp = jnp.concatenate([pcb[:, :, q].reshape(512, 128) for q in range(4)], 1)
            hp = jnp.where(p_kept, hp, 0.0).astype(BF16)
            t_ref[...] = dot(jnp.transpose(hp), hp) * scale + damping(p_kept)
            to_sibling(2)
            rows_over_x()

        @pl.when(b == 1)
        def _():
            columns_over_z()

        @pl.when(b == 2)
        def _():
            rows_over_cores()

        lane_block = lane // 128
        s = dot3(m, t_ref[at, :])
        m_ref[at, :] = jnp.where(lane_block < b, s, 0.0)
        u_ref[at, :] = jnp.where(lane_block > b, s, 0.0)
        m_ref[at, at] = m
        u_ref[at, at] = u
        s_ref[...] = s
        s_ref[:, at] = m

        @pl.when(b < 3)
        def _():
            s = s_ref[...]
            update = dot3(jnp.transpose(s), s)
            row_block = lax.broadcasted_iota(jnp.int32, (512, 1), 0) // 128
            old = t_ref[...]
            t_ref[...] = jnp.where(row_block > b, jnp.where(lane_block == b, 0.0, old) - update, old)

        return 0

    lax.fori_loop(0, 4, factor_block, 0)

    from_sibling(2)
    hp = jnp.concatenate([pcb[:, :, q].reshape(512, 128) for q in range(4)], 1)
    hp = jnp.where(p_kept, hp, 0.0).astype(BF16)
    hpr = jnp.concatenate([pcb[:, :, 4 + q].reshape(512, 128) for q in range(2)], 1)
    hpt = jnp.transpose(hp)
    drain(colb.at[:, :, 1 - z], r_col.at[1])
    hc = jnp.where(kept(j), colb[...].reshape(512, 512), 0.0).astype(BF16)
    hct = jnp.transpose(hc)
    kc = dot(hct, hp) * scale
    cross_c = (dot(hct, hpr) * scale).astype(BF16)
    cross_p = (dot(hpt, hpr) * scale).astype(BF16)
    m = m_ref[...]
    below = (j > p).astype(F32)
    inside = (j == p).astype(F32)
    r = lax.broadcasted_iota(jnp.int32, (512, 512), 0)
    q = lax.broadcasted_iota(jnp.int32, (512, 512), 1)
    fc = dot3(kc, m, 1, 1) * below - jnp.where(r == q, inside, 0.0)
    gh, gl = split(dot3(fc, m))
    outside = 1.0 - inside
    rest = hc.astype(F32) * outside - (dot(hp, gh, 1, 1) + dot(hp, gl, 1, 1))
    rh, rlow = split(rest)
    ch, cl = split(cross_c.astype(F32) * outside - (dot(gh, cross_p) + dot(gl, cross_p)))
    drain(pd.at[:, pl.ds(0, 7)], r_d.at[2])
    chosen_down = pd[...].reshape(256, 512)
    cout[...] = dot(ch, chosen_down) + dot(cl, chosen_down)
    drain(rowb.at[1 - c], r_row.at[3])
    for h in range(2):
        row = 2 * i + h
        r_kept = kept(row)
        hr = jnp.concatenate(
            [
                jnp.concatenate(
                    [rowb[ic, cc, 2 * h + t].reshape(128, 128) for t in range(2) for ic in range(2)], 0
                )
                for cc in range(4)
            ],
            1,
        )
        hrt = jnp.transpose(jnp.where(r_kept, hr, 0.0).astype(BF16))
        under = row > p
        high = jnp.where(under, rh, hc)
        low = jnp.where(under, rlow, jnp.zeros_like(rlow))
        out = (dot(hrt, high) + dot(hrt, low)) * scale
        out = out + damping(r_kept) * (row == j).astype(F32)
        out = jnp.where((row == p) & (j == p), jnp.transpose(u_ref[...]), out)
        fout[512 * h : 512 * h + 512, :] = out

    drain(tok.at[:, pl.ds(0, 15 * 256)], s_tok)
    drain(feat.at[c], s_sib)
    for n, (way, h, hops) in enumerate(CHAINS):
        for s in range(hops - 1):
            drain(sb.at[n, s], s_ch.at[n, s])
        drain(rl.at[n], s_last.at[n])
    drain(zr, s_z)
    drain(xb.at[pl.ds(0, 7)], s_x)
    drain(zb.at[pl.ds(0, 3)], s_zh.at[0])
    drain(zb2.at[pl.ds(0, 3)], s_zh.at[1])
    for n in range(3):
        drain(pcb.at[c, pl.ds(0, 15), panel_part(n)], s_p.at[n])
        drain(pcb.at[c, :, panel_part(n)], s_ps.at[n])
    self_row = (j // 2 == i) & ((j // 2) // 8 == c) & (i // 8 == c)

    @pl.when(self_row)
    def _():
        drain(hpc.at[pl.ds(0, 7)], s_row.at[0])

    @pl.when(jnp.logical_not(self_row))
    def _():
        drain(hpc, s_row.at[0])

    drain(rowb.at[c, x, pl.ds(0, 3)], s_row.at[1])
    drain(rowb.at[c, pl.ds(0, 3)], s_row.at[2])
    drain(part2, s_row.at[3])
    drain(colb.at[:, pl.ds(0, 7), z], s_col.at[0])
    drain(colb.at[:, :, z], s_col.at[1])
    drain(dxr.at[pl.ds(0, 7)], s_d.at[0])
    drain(dzr.at[pl.ds(0, 3)], s_d.at[1])
    drain(pd.at[:, pl.ds(0, 7)], s_d.at[2])


def local(tokens, gate_weight, up_weight, down_weight, pruned_blocks, panel_number):
    vmem = pl.BlockSpec(memory_space=pltpu.VMEM)
    smem = pl.BlockSpec(memory_space=pltpu.SMEM)
    hbm = pl.BlockSpec(memory_space=pl.ANY)
    dma = pltpu.SemaphoreType.DMA

    def b16(*shape):
        return pltpu.VMEM(shape, BF16)

    def f32(*shape):
        return pltpu.VMEM(shape, F32)

    return pl.pallas_call(
        body,
        out_shape=(pltpu.VMEM((1024, 512), F32), pltpu.VMEM((512, 512), F32)),
        in_specs=[hbm] * 4 + [smem] * 2,
        out_specs=(vmem, vmem),
        scratch_shapes=[
            b16(32, 8192), b16(512, 512), b16(512, 512), b16(512, 512),
            b16(2, 8, 64, 256), f32(8, 64, 1024),
            b16(8, 4, 64, 256), b16(8, 3, 64, 256), b16(8, 2, 32, 256),
            b16(32, 1024), b16(32, 1024),
            b16(2, 16, 512), b16(8, 16, 128),
            b16(8, 16, 512),
            b16(4, 16, 128), b16(2, 16, 128), b16(4, 4, 16, 128), b16(4, 2, 16, 128),
            b16(2, 16, 6, 16, 128),
            b16(2, 8, 2, 16, 512), b16(2, 4, 4, 8, 16, 128),
            b16(8, 2, 16, 512), b16(8, 2, 16, 512), b16(2, 16, 512), b16(4, 2, 16, 512), b16(2, 8, 16, 512),
            f32(512, 512), f32(128, 512), f32(512, 512), f32(512, 512),
            dma((4,)), pltpu.SemaphoreType.REGULAR,
            dma, dma((5,)), dma, dma((5,)), dma((8, 3)), dma((8, 3)), dma((8,)), dma((8,)), dma, dma,
            dma, dma, dma((2,)), dma((2,)), dma((3,)), dma((3,)), dma((3,)), dma((3,)),
            dma((4,)), dma((4,)), dma((2,)), dma((2,)), dma((3,)), dma((3,)),
        ],
        compiler_params=pltpu.CompilerParams(
            collective_id=0, has_side_effects=True, vmem_limit_bytes=60 << 20
        ),
        name="prune",
    )(tokens, gate_weight, up_weight, down_weight, pruned_blocks, panel_number)


def solution(mesh):
    in_specs = (P("dp", None), P("dp", "tensor"), P("dp", "tensor"), P("tensor", "dp"), P(), P())
    out_specs = (P("dp", "tensor"), P("tensor", "dp"))
    return jax.shard_map(local, mesh=mesh, in_specs=in_specs, out_specs=out_specs, check_vma=False)
```

```python
import jax
import jax.numpy as jnp
from jax import lax
from jax.experimental import pallas as pl
from jax.experimental.pallas import tpu as pltpu
from jax.sharding import PartitionSpec as P

F32 = jnp.float32
BF16 = jnp.bfloat16
MESH = pl.DeviceIdType.MESH
DAMPING = 0.05
NDP = 16
NT = 32
NY = 8
WIDTH = 8

LONG = ((1, 0, 4), (-1, 2, 4), (1, 1, 4), (-1, 3, 4))
SHORT = ((1, 2, 3), (-1, 0, 3), (1, 3, 3), (-1, 1, 3))
CHAINS = LONG + SHORT


def split(x):
    hi = x.astype(BF16)
    return hi, (x - hi.astype(F32)).astype(BF16)


def dot(a, b, ca=1, cb=0):
    return lax.dot_general(a, b, (((ca,), (cb,)), ((), ())), preferred_element_type=F32)


def dot3(a, b, ca=1, cb=0):
    ah, al = a if isinstance(a, tuple) else split(a)
    bh, bl = b if isinstance(b, tuple) else split(b)
    return dot(ah, bh, ca, cb) + (dot(ah, bl, ca, cb) + dot(al, bh, ca, cb))


def eliminate(t, w, n=128):
    lane = lax.broadcasted_iota(jnp.int32, (1, n), 1)
    nb = w // 2
    m_rows, u_rows = [], []
    for k in range(0, n, w):
        base = n - t.shape[0]
        cols = [jnp.broadcast_to(t[:, k + q : k + q + 1], t.shape) for q in range(w)]
        a = {(r, q): cols[q][k + r - base : k + r - base + 1, :] for r in range(w) for q in range(r + 1)}
        rows = [t[k + q - base : k + q - base + 1, :] for q in range(w)]
        inside = (lane >= k) & (lane < k + w)
        ident = [jnp.where(inside, (lane == k + q).astype(F32), rows[q]) for q in range(w)]
        nxt = (k + w) // 8 * 8
        if k + w < n:
            cols = [col[nxt - base :, :] for col in cols]
            new = jnp.where(inside, 0.0, t[nxt - base :, :])
        for b in range(nb):
            i0, i1 = 2 * b, 2 * b + 1
            p, q, s = a[i0, i0], a[i1, i0], a[i1, i1]
            d = 1.0 / (p * s - q * q)
            ia, ib, ic = s * d, -(q * d), p * d
            r0 = lax.rsqrt(p)
            l = q * r0
            r1 = lax.rsqrt(s - l * l)
            for src, out, keep in ((ident, m_rows, lane < k + w), (rows, u_rows, None)):
                x0 = src[i0] * r0
                x1 = (src[i1] - x0 * l) * r1
                if keep is None:
                    out += [jnp.where(lane >= k + i0, x0, 0.0), jnp.where(lane >= k + i1, x1, 0.0)]
                else:
                    out += [jnp.where(keep, x0, 0.0), jnp.where(keep, x1, 0.0)]
            for r in range(i1 + 1, w):
                f0 = a[r, i0] * ia + a[r, i1] * ib
                f1 = a[r, i0] * ib + a[r, i1] * ic
                for c in range(i1 + 1, r + 1):
                    a[r, c] = a[r, c] - (f0 * a[c, i0] + f1 * a[c, i1])
                if k + w < n:
                    cols[r] = cols[r] - (cols[i0] * f0 + cols[i1] * f1)
                ident[r] = ident[r] - (f0 * ident[i0] + f1 * ident[i1])
                rows[r] = rows[r] - (f0 * rows[i0] + f1 * rows[i1])
            if k + w < n:
                g0 = ident[i0] * ia + ident[i1] * ib
                g1 = ident[i0] * ib + ident[i1] * ic
                new = new - (cols[i0] * g0 + cols[i1] * g1)
        if k + w < n:
            t = new
    return jnp.concatenate(m_rows, 0), jnp.concatenate(u_rows, 0)


def drain(ref, sem):
    pltpu.make_async_copy(ref, ref, sem).wait()


def body(
    tok_in, gate_in, up_in, down_in, pruned, panel,
    fout, cout,
    tok, gate, up, down, feat, pf, sb, rb, rl, zs_own, zr, hch, hpc, xb, zs, zr2, zb, zb2, pcb,
    colb, rowb, dx, dxr, dz, dzr, pd, t_ref, s_ref, m_ref, u_ref, hp_ref, hpt_ref,
    s_in, hello, s_tok, r_tok, s_sib, r_sib, s_ch, r_ch, s_last, r_last, s_z, r_z,
    s_x, r_x, s_zh, r_zh, s_p, r_p, s_ps, r_ps, s_row, r_row, s_col, r_col, s_d, r_d,
):
    i = lax.axis_index("dp")
    j = lax.axis_index("tensor")
    y, z = i // 2, i % 2
    zh, x, c = j // 8, (j // 2) % 4, j % 2
    e8 = j % 8
    sib = j + 1 - 2 * c
    other_z = i + 1 - 2 * z

    def remote(src, dst, send, recv, to):
        pltpu.make_async_remote_copy(
            src_ref=src, dst_ref=dst, send_sem=send, recv_sem=recv, device_id=to, device_id_type=MESH
        ).start()

    def here(src, dst, sem):
        pltpu.make_async_copy(src, dst, sem).start()

    def signal(sem, to):
        pl.semaphore_signal(sem, inc=1, device_id=to, device_id_type=MESH)

    def line(d):
        return j - e8 + (e8 + d) % 8

    for n, (src, dst) in enumerate(((tok_in, tok), (gate_in, gate), (up_in, up), (down_in, down))):
        here(src, dst, s_in.at[n])

    barrier = pltpu.get_barrier_semaphore()

    def greet_dp(d, _):
        signal(barrier, ((i + d) % NDP, j))
        return 0

    def greet_line(d, _):
        signal(barrier, (i, line(d)))
        return 0

    def greet_zh(d, _):
        signal(barrier, (i, (j + 8 * d) % NT))
        return 0

    lax.fori_loop(1, NDP, greet_dp, 0)
    lax.fori_loop(1, 4, greet_zh, 0)
    lax.fori_loop(1, 8, greet_line, 0)
    drain(tok, s_in.at[0])
    pl.semaphore_wait(barrier, NDP - 1 + 3 + 7)

    def send_tok(o, g):
        src = tok.at[:, pl.ds(pl.multiple_of(512 * o + 256 * c, 256), 256)]
        dst = feat.at[c, y, pl.ds(pl.multiple_of(32 * z, 32), 32), :]
        remote(src, dst, s_tok, r_tok.at[g], (o, j))

    for g in (4, 3, 2, 1, 0):
        for way in (1, -1) if g in (1, 2, 3) else (1,):
            yo = (y + way * g + NY) % NY
            for zo in (z, 1 - z):
                if g == 0 and zo is z:
                    src = tok.at[:, pl.ds(pl.multiple_of(512 * i + 256 * c, 256), 256)]
                    here(src, feat.at[c, y, pl.ds(pl.multiple_of(32 * z, 32), 32), :], r_tok.at[0])
                else:
                    send_tok(2 * yo + zo, g)
    for d in range(1, 4):
        signal(hello, (i, (j + 8 * d) % NT))

    drain(down, s_in.at[3])
    for n in range(2):
        quarter = pruned[n] % 4
        for e in range(8):
            rows = [down[128 * k + 16 * e : 128 * k + 16 * e + 16, :] for k in range(4)]
            low = jnp.where(quarter == 0, rows[0], rows[1])
            high = jnp.where(quarter == 2, rows[2], rows[3])
            dx[e, n] = jnp.where(quarter < 2, low, high)

    def send_dx(d, _):
        e = (e8 + d) % 8
        remote(dx.at[e], dxr.at[e8], s_d.at[0], r_d.at[0], (i, line(d)))
        return 0

    lax.fori_loop(1, 8, send_dx, 0)
    here(dx.at[e8], dxr.at[e8], r_d.at[0])

    def blocks(g):
        return ((y + g) % NY, (y + NY - g) % NY) if g in (1, 2, 3) else ((y + g) % NY,)

    def forward(g):
        drain(feat.at[c, pl.ds(0, len(blocks(g)))], r_tok.at[g])
        for yb in blocks(g):
            remote(feat.at[c, yb], feat.at[c, yb], s_sib, r_sib.at[g], (i, sib))

    drain(gate, s_in.at[1])
    drain(up, s_in.at[2])

    def multiply(g):
        bs = blocks(g)
        drain(feat.at[c, pl.ds(0, len(bs))], r_sib.at[g])
        halves = [jnp.concatenate([feat[k, yb] for yb in bs], 0) for k in range(2)]
        for h, w in enumerate((gate, up)):
            v = dot(halves[0], w[:256, :]) + dot(halves[1], w[256:, :])
            for k, yb in enumerate(bs):
                pf[yb, :, 512 * h : 512 * h + 512] = v[64 * k : 64 * k + 64]

    def chain(n, s):
        way, h, hops = CHAINS[n]
        yd = (y + way * (hops - s + 1) + NY) % NY
        v = pf[yd, :, 256 * h : 256 * h + 256]
        if s > 1:
            drain(rb.at[n, s - 2], r_ch.at[n, s - 2])
            v = v + rb[n, s - 2].astype(F32)
        sb[n, s - 1] = v.astype(BF16)
        to = 2 * ((y + way + NY) % NY)
        if s < hops:
            remote(sb.at[n, s - 1], rb.at[n, s - 1], s_ch.at[n, s - 1], r_ch.at[n, s - 1], (to + z, j))
        else:
            for zo in (z, 1 - z):
                part = sb.at[n, s - 1, pl.ds(pl.multiple_of(32 * zo, 32), 32), :]
                remote(part, rl.at[n, z], s_last.at[n], r_last.at[n], (to + zo, j))

    def long(s):
        for n in range(4):
            chain(n, s)

    def short(s):
        for n in range(4, 8):
            chain(n, s)

    pl.semaphore_wait(hello, 3)
    forward(4)
    forward(3)
    multiply(4)
    long(1)
    forward(2)
    multiply(3)
    short(1)
    forward(1)
    multiply(2)
    long(2)
    drain(dxr, r_d.at[0])
    for n in range(2):
        dz[n] = dxr[(pruned[n] // 4) % 8, n]
    for d in range(1, 4):
        remote(dz, dzr.at[zh], s_d.at[1], r_d.at[1], (i, (j + 8 * d) % NT))
    here(dz, dzr.at[zh], r_d.at[1])
    short(2)
    forward(0)
    multiply(1)
    long(3)
    multiply(0)
    own_rows = pl.ds(pl.multiple_of(32 * z, 32), 32)
    zs_own[...] = pf[y, pl.ds(pl.multiple_of(32 * (1 - z), 32), 32), :].astype(BF16)
    remote(zs_own, zr, s_z, r_z, (other_z, j))
    short(3)
    long(4)
    drain(zr, r_z)
    total = []
    for h in range(2):
        quarters = []
        for k in (2 * h, 2 * h + 1):
            v = pf[y, own_rows, 256 * k : 256 * k + 256] + zr[:, 256 * k : 256 * k + 256].astype(F32)
            for n in (4, 5, 6, 7, 0, 1, 2, 3):
                if CHAINS[n][1] == k:
                    drain(rl.at[n], r_last.at[n])
                    v = v + (rl[n, 0].astype(F32) + rl[n, 1].astype(F32))
            quarters.append(v)
        total.append(jnp.concatenate(quarters, 1))
    g, u = total
    hidden = (g / (1.0 + jnp.exp(-g)) * u).astype(BF16)
    for t in range(2):
        hch[t] = hidden[16 * t : 16 * t + 16, :]

    def send_x(d, _):
        e = (e8 + d) % 8
        remote(hch.at[e % 2], xb.at[e8], s_x, r_x, (i, line(d)))
        return 0

    lax.fori_loop(1, 8, send_x, 0)
    here(hch.at[c], xb.at[e8], r_x)

    for t in range(2):
        for q in range(4):
            hpc[4 * t + q] = hidden[16 * t : 16 * t + 16, 128 * q : 128 * q + 128]

    def send_row(q, _):
        k = 8 * c + q
        ic = i // 8
        dst = rowb.at[ic, q % 4, 2 * c + q // 4, i % 8]
        same = (j // 2 == i) & (2 * k + ic == j)

        @pl.when(same)
        def _():
            here(hpc.at[q], dst, r_row.at[0])

        @pl.when(jnp.logical_not(same))
        def _():
            remote(hpc.at[q], dst, s_row.at[0], r_row.at[0], (j // 2, 2 * k + ic))

        return 0

    lax.fori_loop(0, 8, send_row, 0)

    drain(dzr, r_d.at[1])
    for n in range(2):
        pd[n, e8] = dzr[pruned[n] // 32, n]

    def send_pd(d, _):
        remote(pd.at[:, e8], pd.at[:, e8], s_d.at[2], r_d.at[2], (i, line(d)))
        return 0

    lax.fori_loop(1, 8, send_pd, 0)

    drain(xb, r_x)
    chosen = xb[panel[0] % 8]
    for q in range(4):
        zs[q] = chosen[:, 128 * q : 128 * q + 128]
    for d in range(1, 4):
        remote(zs, zb.at[zh], s_zh.at[0], r_zh.at[0], (i, (j + 8 * d) % NT))
    here(zs, zb.at[zh], r_zh.at[0])
    for n in range(2):
        quarter = pruned[n] % 4
        rows = [xb[(pruned[n] // 4) % 8, :, 128 * k : 128 * k + 128] for k in range(4)]
        low = jnp.where(quarter == 0, rows[0], rows[1])
        high = jnp.where(quarter == 2, rows[2], rows[3])
        zr2[n] = jnp.where(quarter < 2, low, high)
    for d in range(1, 4):
        remote(zr2, zb2.at[zh], s_zh.at[1], r_zh.at[1], (i, (j + 8 * d) % NT))
    here(zr2, zb2.at[zh], r_zh.at[1])

    def send_dp(part, n):
        def one(d, _):
            remote(part, part, s_p.at[n], r_p.at[n], ((i + d) % NDP, j))
            return 0

        lax.fori_loop(1, NDP, one, 0)

    def panel_part(n):
        return (pl.ds(0, 1), pl.ds(1, 3), pl.ds(4, 2))[n]

    drain(zb, r_zh.at[0])
    for q in range(4):
        pcb[c, i, q] = zb[panel[0] // 8, q]
    send_dp(pcb.at[c, i, panel_part(0)], 0)
    send_dp(pcb.at[c, i, panel_part(1)], 1)
    drain(zb2, r_zh.at[1])
    for n in range(2):
        pcb[c, i, 4 + n] = zb2[pruned[n] // 32, n]
    send_dp(pcb.at[c, i, panel_part(2)], 2)

    def send_col(d, _):
        remote(hch, colb.at[:, y, z], s_col.at[0], r_col.at[0], (2 * ((y + d) % NY) + z, j))
        return 0

    lax.fori_loop(1, NY, send_col, 0)
    here(hch, colb.at[:, y, z], r_col.at[0])

    def columns_over_z():
        same_z = colb.at[:, :, z]
        drain(same_z, r_col.at[0])
        remote(same_z, same_z, s_col.at[1], r_col.at[1], (other_z, j))

    def to_sibling(n):
        part = panel_part(n)
        drain(pcb.at[c, pl.ds(0, 15), part], r_p.at[n])
        remote(pcb.at[c, :, part], pcb.at[c, :, part], s_ps.at[n], r_ps.at[n], (i, sib))

    def from_sibling(n):
        drain(pcb.at[1 - c, :, panel_part(n)], r_ps.at[n])

    part0 = rowb.at[c, x, zh]
    part1 = rowb.at[c, x]
    part2 = rowb.at[c]

    def rows_over_z():
        drain(part0, r_row.at[0])
        for d in range(1, 4):
            remote(part0, part0, s_row.at[1], r_row.at[1], (i, (j + 8 * d) % NT))

    def rows_over_x():
        drain(rowb.at[c, x, pl.ds(0, 3)], r_row.at[1])
        for d in range(1, 4):
            remote(part1, part1, s_row.at[2], r_row.at[2], (i, zh * 8 + ((x + d) % 4) * 2 + c))

    def rows_over_cores():
        drain(rowb.at[c, pl.ds(0, 3)], r_row.at[2])
        remote(part2, part2, s_row.at[3], r_row.at[3], (i, sib))

    to_sibling(0)
    rows_over_z()

    lane = lax.broadcasted_iota(jnp.int32, (1, 512), 1)
    scale = 1.0 / 512
    b0, b1 = pruned[0], pruned[1]
    p = panel[0]

    def kept(block512):
        blk = block512 * 4 + lane // 128
        return (blk != b0) & (blk != b1)

    def damping(keep):
        n = keep.shape[1]
        r = lax.broadcasted_iota(jnp.int32, (n, n), 0)
        q = lax.broadcasted_iota(jnp.int32, (n, n), 1)
        return jnp.where(r == q, jnp.where(keep, DAMPING, 1.0), 0.0)

    p_kept = kept(p)
    from_sibling(0)
    hp0 = jnp.where(p_kept[:, :128], pcb[:, :, 0].reshape(512, 128), 0.0).astype(BF16)
    t_ref[:128, :128] = dot(jnp.transpose(hp0), hp0) * scale + damping(p_kept[:, :128])

    def factor_block(b, _):
        s0 = pl.multiple_of(128 * b, 128)
        at = pl.ds(s0, 128)
        m, u = eliminate(t_ref[at, at], WIDTH)

        @pl.when(b == 0)
        def _():
            to_sibling(1)
            from_sibling(1)
            hp = jnp.concatenate([pcb[:, :, q].reshape(512, 128) for q in range(4)], 1)
            hp = jnp.where(p_kept, hp, 0.0).astype(BF16)
            hp_ref[...] = hp
            hpt = jnp.transpose(hp)
            hpt_ref[...] = hpt
            t_ref[...] = dot(hpt, hp) * scale + damping(p_kept)
            to_sibling(2)
            rows_over_x()

        @pl.when(b == 1)
        def _():
            columns_over_z()

        @pl.when(b == 2)
        def _():
            rows_over_cores()

        lane_block = lane // 128
        s = dot3(m, t_ref[at, :])
        m_ref[at, :] = jnp.where(lane_block < b, s, 0.0)
        u_ref[at, :] = jnp.where(lane_block > b, s, 0.0)
        m_ref[at, at] = m
        u_ref[at, at] = u
        s_ref[...] = s
        s_ref[:, at] = m

        for k in range(3):

            @pl.when(b == k)
            def _():
                under = slice(128 * k + 128, 512)
                parts = split(s_ref[...])
                left = tuple(jnp.transpose(v[:, under]) for v in parts)
                update = dot3(left, parts)
                t_ref[under, under] -= update[:, under]
                t_ref[under, : 128 * k + 128] = (
                    jnp.where(lane[:, : 128 * k + 128] < 128 * k, t_ref[under, : 128 * k + 128], 0.0)
                    - update[:, : 128 * k + 128]
                )

        return 0

    lax.fori_loop(0, 4, factor_block, 0)

    from_sibling(2)
    hp = hp_ref[...]
    hpr = jnp.concatenate([pcb[:, :, 4 + q].reshape(512, 128) for q in range(2)], 1)
    hpt = hpt_ref[...]
    drain(colb.at[:, :, 1 - z], r_col.at[1])
    hc = jnp.where(kept(j), colb[...].reshape(512, 512), 0.0).astype(BF16)
    hct = jnp.transpose(hc)
    below = (j > p).astype(F32)
    inside = (j == p).astype(F32)
    kc = dot(hct, hp) * (scale * below)
    cross_c = (dot(hct, hpr) * scale).astype(BF16)
    cross_p = (dot(hpt, hpr) * scale).astype(BF16)
    m_parts = split(m_ref[...])
    r = lax.broadcasted_iota(jnp.int32, (128, 128), 0)
    q = lax.broadcasted_iota(jnp.int32, (128, 128), 1)
    t_ref[...] = dot3(kc, m_parts, 1, 1)
    for k in range(4):
        at = slice(128 * k, 128 * k + 128)
        t_ref[at, at] -= jnp.where(r == q, inside, 0.0)
    gh, gl = split(dot3(t_ref[...], m_parts))
    outside = 1.0 - inside
    rest = hc.astype(F32) * outside - (dot(hp, gh, 1, 1) + dot(hp, gl, 1, 1))
    rh, rlow = split(rest)
    ch, cl = split(cross_c.astype(F32) * outside - (dot(gh, cross_p) + dot(gl, cross_p)))
    drain(pd.at[:, pl.ds(0, 7)], r_d.at[2])
    chosen_down = pd[...].reshape(256, 512)
    cout[...] = dot(ch, chosen_down) + dot(cl, chosen_down)
    drain(rowb.at[1 - c], r_row.at[3])
    lower = jnp.transpose(u_ref[...])
    for h in range(2):
        row = 2 * i + h
        r_kept = kept(row)
        hr = jnp.concatenate(
            [
                jnp.concatenate(
                    [rowb[ic, cc, 2 * h + t].reshape(128, 128) for t in range(2) for ic in range(2)], 0
                )
                for cc in range(4)
            ],
            1,
        )
        hrt = jnp.transpose(jnp.where(r_kept, hr, 0.0).astype(BF16))
        under = row > p
        high = jnp.where(under, rh, hc)
        low = jnp.where(under, rlow, jnp.zeros_like(rlow))
        out = (dot(hrt, high) + dot(hrt, low)) * scale
        rows = slice(512 * h, 512 * h + 512)
        fout[rows, :] = jnp.where((row == p) & (j == p), lower, out)
        on_diagonal = ((row == j) & (row != p)).astype(F32)
        for k in range(4):
            at = slice(128 * k, 128 * k + 128)
            rows = slice(512 * h + 128 * k, 512 * h + 128 * k + 128)
            fout[rows, at] += damping(r_kept[:, at]) * on_diagonal

    drain(tok.at[:, pl.ds(0, 15 * 256)], s_tok)
    drain(feat.at[c], s_sib)
    for n, (way, h, hops) in enumerate(CHAINS):
        for s in range(hops - 1):
            drain(sb.at[n, s], s_ch.at[n, s])
        drain(rl.at[n], s_last.at[n])
    drain(zr, s_z)
    drain(xb.at[pl.ds(0, 7)], s_x)
    drain(zb.at[pl.ds(0, 3)], s_zh.at[0])
    drain(zb2.at[pl.ds(0, 3)], s_zh.at[1])
    for n in range(3):
        drain(pcb.at[c, pl.ds(0, 15), panel_part(n)], s_p.at[n])
        drain(pcb.at[c, :, panel_part(n)], s_ps.at[n])
    self_row = (j // 2 == i) & ((j // 2) // 8 == c) & (i // 8 == c)

    @pl.when(self_row)
    def _():
        drain(hpc.at[pl.ds(0, 7)], s_row.at[0])

    @pl.when(jnp.logical_not(self_row))
    def _():
        drain(hpc, s_row.at[0])

    drain(rowb.at[c, x, pl.ds(0, 3)], s_row.at[1])
    drain(rowb.at[c, pl.ds(0, 3)], s_row.at[2])
    drain(part2, s_row.at[3])
    drain(colb.at[:, pl.ds(0, 7), z], s_col.at[0])
    drain(colb.at[:, :, z], s_col.at[1])
    drain(dxr.at[pl.ds(0, 7)], s_d.at[0])
    drain(dzr.at[pl.ds(0, 3)], s_d.at[1])
    drain(pd.at[:, pl.ds(0, 7)], s_d.at[2])


def local(tokens, gate_weight, up_weight, down_weight, pruned_blocks, panel_number):
    vmem = pl.BlockSpec(memory_space=pltpu.VMEM)
    smem = pl.BlockSpec(memory_space=pltpu.SMEM)
    hbm = pl.BlockSpec(memory_space=pl.ANY)
    dma = pltpu.SemaphoreType.DMA

    def b16(*shape):
        return pltpu.VMEM(shape, BF16)

    def f32(*shape):
        return pltpu.VMEM(shape, F32)

    return pl.pallas_call(
        body,
        out_shape=(pltpu.VMEM((1024, 512), F32), pltpu.VMEM((512, 512), F32)),
        in_specs=[hbm] * 4 + [smem] * 2,
        out_specs=(vmem, vmem),
        scratch_shapes=[
            b16(32, 8192), b16(512, 512), b16(512, 512), b16(512, 512),
            b16(2, 8, 64, 256), f32(8, 64, 1024),
            b16(8, 4, 64, 256), b16(8, 3, 64, 256), b16(8, 2, 32, 256),
            b16(32, 1024), b16(32, 1024),
            b16(2, 16, 512), b16(8, 16, 128),
            b16(8, 16, 512),
            b16(4, 16, 128), b16(2, 16, 128), b16(4, 4, 16, 128), b16(4, 2, 16, 128),
            b16(2, 16, 6, 16, 128),
            b16(2, 8, 2, 16, 512), b16(2, 4, 4, 8, 16, 128),
            b16(8, 2, 16, 512), b16(8, 2, 16, 512), b16(2, 16, 512), b16(4, 2, 16, 512), b16(2, 8, 16, 512),
            f32(512, 512), f32(128, 512), f32(512, 512), f32(512, 512),
            b16(512, 512), b16(512, 512),
            dma((4,)), pltpu.SemaphoreType.REGULAR,
            dma, dma((5,)), dma, dma((5,)), dma((8, 3)), dma((8, 3)), dma((8,)), dma((8,)), dma, dma,
            dma, dma, dma((2,)), dma((2,)), dma((3,)), dma((3,)), dma((3,)), dma((3,)),
            dma((4,)), dma((4,)), dma((2,)), dma((2,)), dma((3,)), dma((3,)),
        ],
        compiler_params=pltpu.CompilerParams(
            collective_id=0, has_side_effects=True, vmem_limit_bytes=60 << 20
        ),
        name="prune",
    )(tokens, gate_weight, up_weight, down_weight, pruned_blocks, panel_number)


def solution(mesh):
    in_specs = (P("dp", None), P("dp", "tensor"), P("dp", "tensor"), P("tensor", "dp"), P(), P())
    out_specs = (P("dp", "tensor"), P("tensor", "dp"))
    return jax.shard_map(local, mesh=mesh, in_specs=in_specs, out_specs=out_specs, check_vma=False)
```

```python
import jax
import jax.numpy as jnp
from jax import lax
from jax.experimental import pallas as pl
from jax.experimental.pallas import tpu as pltpu
from jax.sharding import PartitionSpec as P

F32 = jnp.float32
BF16 = jnp.bfloat16
MESH = pl.DeviceIdType.MESH
DAMPING = 0.05
NDP = 16
NT = 32
NY = 8
WIDTH = 8

LONG = ((1, 0, 4), (-1, 2, 4), (1, 1, 4), (-1, 3, 4))
SHORT = ((1, 2, 3), (-1, 0, 3), (1, 3, 3), (-1, 1, 3))
CHAINS = LONG + SHORT


def split(x):
    hi = x.astype(BF16)
    return hi, (x - hi.astype(F32)).astype(BF16)


def dot(a, b, ca=1, cb=0):
    return lax.dot_general(a, b, (((ca,), (cb,)), ((), ())), preferred_element_type=F32)


def dot3(a, b, ca=1, cb=0):
    ah, al = a if isinstance(a, tuple) else split(a)
    bh, bl = b if isinstance(b, tuple) else split(b)
    return dot(ah, bh, ca, cb) + (dot(ah, bl, ca, cb) + dot(al, bh, ca, cb))


def eliminate(t, w, n=128):
    lane = lax.broadcasted_iota(jnp.int32, (1, n), 1)
    nb = w // 2
    m_rows, u_rows = [], []
    for k in range(0, n, w):
        base = n - t.shape[0]
        cols = [jnp.broadcast_to(t[:, k + q : k + q + 1], t.shape) for q in range(w)]
        a = {(r, q): cols[q][k + r - base : k + r - base + 1, :] for r in range(w) for q in range(r + 1)}
        rows = [t[k + q - base : k + q - base + 1, :] for q in range(w)]
        inside = (lane >= k) & (lane < k + w)
        ident = [jnp.where(inside, (lane == k + q).astype(F32), rows[q]) for q in range(w)]
        nxt = (k + w) // 8 * 8
        if k + w < n:
            cols = [col[nxt - base :, :] for col in cols]
            new = jnp.where(inside, 0.0, t[nxt - base :, :])
        for b in range(nb):
            i0, i1 = 2 * b, 2 * b + 1
            p, q, s = a[i0, i0], a[i1, i0], a[i1, i1]
            d = 1.0 / (p * s - q * q)
            ia, ib, ic = s * d, -(q * d), p * d
            r0 = lax.rsqrt(p)
            l = q * r0
            r1 = lax.rsqrt(s - l * l)
            for src, out, keep in ((ident, m_rows, lane < k + w), (rows, u_rows, None)):
                x0 = src[i0] * r0
                x1 = (src[i1] - x0 * l) * r1
                if keep is None:
                    out += [jnp.where(lane >= k + i0, x0, 0.0), jnp.where(lane >= k + i1, x1, 0.0)]
                else:
                    out += [jnp.where(keep, x0, 0.0), jnp.where(keep, x1, 0.0)]
            for r in range(i1 + 1, w):
                f0 = a[r, i0] * ia + a[r, i1] * ib
                f1 = a[r, i0] * ib + a[r, i1] * ic
                for c in range(i1 + 1, r + 1):
                    a[r, c] = a[r, c] - (f0 * a[c, i0] + f1 * a[c, i1])
                if k + w < n:
                    cols[r] = cols[r] - (cols[i0] * f0 + cols[i1] * f1)
                ident[r] = ident[r] - (f0 * ident[i0] + f1 * ident[i1])
                rows[r] = rows[r] - (f0 * rows[i0] + f1 * rows[i1])
            if k + w < n:
                g0 = ident[i0] * ia + ident[i1] * ib
                g1 = ident[i0] * ib + ident[i1] * ic
                new = new - (cols[i0] * g0 + cols[i1] * g1)
        if k + w < n:
            t = new
    return jnp.concatenate(m_rows, 0), jnp.concatenate(u_rows, 0)


def drain(ref, sem):
    pltpu.make_async_copy(ref, ref, sem).wait()


def body(
    tok_in, gate_in, up_in, down_in, pruned, panel,
    fout, cout,
    tok, gate, up, down, feat, pf, sb, sl, rb, rl, zs_own, zr, hch, hpc, xb, zs, zr2, zb, zb2, pcb,
    colb, rowb, dx, dxr, dz, dzr, pd, t_ref, s_ref, m_ref, u_ref, hp_ref, hpt_ref,
    s_in, hello, s_tok, r_tok, s_sib, r_sib, s_ch, r_ch, s_last, r_last, s_z, r_z,
    s_x, r_x, s_zh, r_zh, s_p, r_p, s_ps, r_ps, s_row, r_row, s_col, r_col, s_d, r_d,
):
    i = lax.axis_index("dp")
    j = lax.axis_index("tensor")
    y, z = i // 2, i % 2
    zh, x, c = j // 8, (j // 2) % 4, j % 2
    e8 = j % 8
    sib = j + 1 - 2 * c
    other_z = i + 1 - 2 * z

    def remote(src, dst, send, recv, to):
        pltpu.make_async_remote_copy(
            src_ref=src, dst_ref=dst, send_sem=send, recv_sem=recv, device_id=to, device_id_type=MESH
        ).start()

    def here(src, dst, sem):
        pltpu.make_async_copy(src, dst, sem).start()

    def signal(sem, to):
        pl.semaphore_signal(sem, inc=1, device_id=to, device_id_type=MESH)

    def line(d):
        return j - e8 + (e8 + d) % 8

    for n, (src, dst) in enumerate(((tok_in, tok), (gate_in, gate), (up_in, up), (down_in, down))):
        here(src, dst, s_in.at[n])

    barrier = pltpu.get_barrier_semaphore()

    def greet_dp(d, _):
        signal(barrier, ((i + d) % NDP, j))
        return 0

    def greet_line(d, _):
        signal(barrier, (i, line(d)))
        return 0

    def greet_zh(d, _):
        signal(barrier, (i, (j + 8 * d) % NT))
        return 0

    lax.fori_loop(1, NDP, greet_dp, 0)
    lax.fori_loop(1, 4, greet_zh, 0)
    lax.fori_loop(1, 8, greet_line, 0)
    drain(tok, s_in.at[0])
    pl.semaphore_wait(barrier, NDP - 1 + 3 + 7)

    def send_tok(o, g):
        src = tok.at[:, pl.ds(pl.multiple_of(512 * o + 256 * c, 256), 256)]
        dst = feat.at[c, y, pl.ds(pl.multiple_of(32 * z, 32), 32), :]
        remote(src, dst, s_tok, r_tok.at[g], (o, j))

    for g in (4, 3, 2, 1, 0):
        for way in (1, -1) if g in (1, 2, 3) else (1,):
            yo = (y + way * g + NY) % NY
            for zo in (z, 1 - z):
                if g == 0 and zo is z:
                    src = tok.at[:, pl.ds(pl.multiple_of(512 * i + 256 * c, 256), 256)]
                    here(src, feat.at[c, y, pl.ds(pl.multiple_of(32 * z, 32), 32), :], r_tok.at[0])
                else:
                    send_tok(2 * yo + zo, g)
    for d in range(1, 4):
        signal(hello, (i, (j + 8 * d) % NT))

    drain(down, s_in.at[3])
    for n in range(2):
        quarter = pruned[n] % 4
        for e in range(8):
            rows = [down[128 * k + 16 * e : 128 * k + 16 * e + 16, :] for k in range(4)]
            low = jnp.where(quarter == 0, rows[0], rows[1])
            high = jnp.where(quarter == 2, rows[2], rows[3])
            dx[e, n] = jnp.where(quarter < 2, low, high)

    def send_dx(d, _):
        e = (e8 + d) % 8
        remote(dx.at[e], dxr.at[e8], s_d.at[0], r_d.at[0], (i, line(d)))
        return 0

    lax.fori_loop(1, 8, send_dx, 0)
    here(dx.at[e8], dxr.at[e8], r_d.at[0])

    def blocks(g):
        return ((y + g) % NY, (y + NY - g) % NY) if g in (1, 2, 3) else ((y + g) % NY,)

    def forward(g):
        drain(feat.at[c, pl.ds(0, len(blocks(g)))], r_tok.at[g])
        for yb in blocks(g):
            remote(feat.at[c, yb], feat.at[c, yb], s_sib, r_sib.at[g], (i, sib))

    drain(gate, s_in.at[1])
    drain(up, s_in.at[2])

    def multiply(g):
        bs = blocks(g)
        drain(feat.at[c, pl.ds(0, len(bs))], r_sib.at[g])
        halves = [jnp.concatenate([feat[k, yb] for yb in bs], 0) for k in range(2)]
        for h, w in enumerate((gate, up)):
            v = dot(halves[0], w[:256, :]) + dot(halves[1], w[256:, :])
            for k, yb in enumerate(bs):
                pf[yb, :, 512 * h : 512 * h + 512] = v[64 * k : 64 * k + 64]

    def chain(n, s):
        way, h, hops = CHAINS[n]
        yd = (y + way * (hops - s + 1) + NY) % NY
        v = pf[yd, :, 256 * h : 256 * h + 256]
        if s > 1:
            drain(rb.at[n, s - 2], r_ch.at[n, s - 2])
            v = v + rb[n, s - 2].astype(F32)
        if s < hops:
            sb[n, s - 1] = v.astype(BF16)
        else:
            sl[n] = v
        to = 2 * ((y + way + NY) % NY)
        if s < hops:
            remote(sb.at[n, s - 1], rb.at[n, s - 1], s_ch.at[n, s - 1], r_ch.at[n, s - 1], (to + z, j))
        else:
            for zo in (z, 1 - z):
                part = sl.at[n, pl.ds(pl.multiple_of(32 * zo, 32), 32), :]
                remote(part, rl.at[n, z], s_last.at[n], r_last.at[n], (to + zo, j))

    def long(s):
        for n in range(4):
            chain(n, s)

    def short(s):
        for n in range(4, 8):
            chain(n, s)

    pl.semaphore_wait(hello, 3)
    forward(4)
    forward(3)
    multiply(4)
    long(1)
    forward(2)
    multiply(3)
    short(1)
    forward(1)
    multiply(2)
    long(2)
    drain(dxr, r_d.at[0])
    for n in range(2):
        dz[n] = dxr[(pruned[n] // 4) % 8, n]
    for d in range(1, 4):
        remote(dz, dzr.at[zh], s_d.at[1], r_d.at[1], (i, (j + 8 * d) % NT))
    here(dz, dzr.at[zh], r_d.at[1])
    short(2)
    forward(0)
    multiply(1)
    long(3)
    multiply(0)
    own_rows = pl.ds(pl.multiple_of(32 * z, 32), 32)
    zs_own[...] = pf[y, pl.ds(pl.multiple_of(32 * (1 - z), 32), 32), :].astype(BF16)
    remote(zs_own, zr, s_z, r_z, (other_z, j))
    short(3)
    long(4)
    drain(zr, r_z)
    total = []
    for h in range(2):
        quarters = []
        for k in (2 * h, 2 * h + 1):
            v = pf[y, own_rows, 256 * k : 256 * k + 256] + zr[:, 256 * k : 256 * k + 256].astype(F32)
            for n in (4, 5, 6, 7, 0, 1, 2, 3):
                if CHAINS[n][1] == k:
                    drain(rl.at[n], r_last.at[n])
                    v = v + (rl[n, 0] + rl[n, 1])
            quarters.append(v)
        total.append(jnp.concatenate(quarters, 1))
    g, u = total
    hidden = (g / (1.0 + jnp.exp(-g)) * u).astype(BF16)
    for t in range(2):
        hch[t] = hidden[16 * t : 16 * t + 16, :]

    def send_x(d, _):
        e = (e8 + d) % 8
        remote(hch.at[e % 2], xb.at[e8], s_x, r_x, (i, line(d)))
        return 0

    lax.fori_loop(1, 8, send_x, 0)
    here(hch.at[c], xb.at[e8], r_x)

    for t in range(2):
        for q in range(4):
            hpc[4 * t + q] = hidden[16 * t : 16 * t + 16, 128 * q : 128 * q + 128]

    def send_row(q, _):
        k = 8 * c + q
        ic = i // 8
        dst = rowb.at[ic, q % 4, 2 * c + q // 4, i % 8]
        same = (j // 2 == i) & (2 * k + ic == j)

        @pl.when(same)
        def _():
            here(hpc.at[q], dst, r_row.at[0])

        @pl.when(jnp.logical_not(same))
        def _():
            remote(hpc.at[q], dst, s_row.at[0], r_row.at[0], (j // 2, 2 * k + ic))

        return 0

    lax.fori_loop(0, 8, send_row, 0)

    drain(dzr, r_d.at[1])
    for n in range(2):
        pd[n, e8] = dzr[pruned[n] // 32, n]

    def send_pd(d, _):
        remote(pd.at[:, e8], pd.at[:, e8], s_d.at[2], r_d.at[2], (i, line(d)))
        return 0

    lax.fori_loop(1, 8, send_pd, 0)

    drain(xb, r_x)
    chosen = xb[panel[0] % 8]
    for q in range(4):
        zs[q] = chosen[:, 128 * q : 128 * q + 128]
    for d in range(1, 4):
        remote(zs, zb.at[zh], s_zh.at[0], r_zh.at[0], (i, (j + 8 * d) % NT))
    here(zs, zb.at[zh], r_zh.at[0])
    for n in range(2):
        quarter = pruned[n] % 4
        rows = [xb[(pruned[n] // 4) % 8, :, 128 * k : 128 * k + 128] for k in range(4)]
        low = jnp.where(quarter == 0, rows[0], rows[1])
        high = jnp.where(quarter == 2, rows[2], rows[3])
        zr2[n] = jnp.where(quarter < 2, low, high)
    for d in range(1, 4):
        remote(zr2, zb2.at[zh], s_zh.at[1], r_zh.at[1], (i, (j + 8 * d) % NT))
    here(zr2, zb2.at[zh], r_zh.at[1])

    def send_dp(part, n):
        def one(d, _):
            remote(part, part, s_p.at[n], r_p.at[n], ((i + d) % NDP, j))
            return 0

        lax.fori_loop(1, NDP, one, 0)

    def panel_part(n):
        return (pl.ds(0, 1), pl.ds(1, 3), pl.ds(4, 2))[n]

    drain(zb, r_zh.at[0])
    for q in range(4):
        pcb[c, i, q] = zb[panel[0] // 8, q]
    send_dp(pcb.at[c, i, panel_part(0)], 0)
    send_dp(pcb.at[c, i, panel_part(1)], 1)
    drain(zb2, r_zh.at[1])
    for n in range(2):
        pcb[c, i, 4 + n] = zb2[pruned[n] // 32, n]
    send_dp(pcb.at[c, i, panel_part(2)], 2)

    def send_col(d, _):
        remote(hch, colb.at[:, y, z], s_col.at[0], r_col.at[0], (2 * ((y + d) % NY) + z, j))
        return 0

    lax.fori_loop(1, NY, send_col, 0)
    here(hch, colb.at[:, y, z], r_col.at[0])

    def columns_over_z():
        same_z = colb.at[:, :, z]
        drain(same_z, r_col.at[0])
        remote(same_z, same_z, s_col.at[1], r_col.at[1], (other_z, j))

    def to_sibling(n):
        part = panel_part(n)
        drain(pcb.at[c, pl.ds(0, 15), part], r_p.at[n])
        remote(pcb.at[c, :, part], pcb.at[c, :, part], s_ps.at[n], r_ps.at[n], (i, sib))

    def from_sibling(n):
        drain(pcb.at[1 - c, :, panel_part(n)], r_ps.at[n])

    part0 = rowb.at[c, x, zh]
    part1 = rowb.at[c, x]
    part2 = rowb.at[c]

    def rows_over_z():
        drain(part0, r_row.at[0])
        for d in range(1, 4):
            remote(part0, part0, s_row.at[1], r_row.at[1], (i, (j + 8 * d) % NT))

    def rows_over_x():
        drain(rowb.at[c, x, pl.ds(0, 3)], r_row.at[1])
        for d in range(1, 4):
            remote(part1, part1, s_row.at[2], r_row.at[2], (i, zh * 8 + ((x + d) % 4) * 2 + c))

    def rows_over_cores():
        drain(rowb.at[c, pl.ds(0, 3)], r_row.at[2])
        remote(part2, part2, s_row.at[3], r_row.at[3], (i, sib))

    to_sibling(0)
    rows_over_z()

    lane = lax.broadcasted_iota(jnp.int32, (1, 512), 1)
    scale = 1.0 / 512
    b0, b1 = pruned[0], pruned[1]
    p = panel[0]

    def kept(block512):
        blk = block512 * 4 + lane // 128
        return (blk != b0) & (blk != b1)

    def damping(keep):
        n = keep.shape[1]
        r = lax.broadcasted_iota(jnp.int32, (n, n), 0)
        q = lax.broadcasted_iota(jnp.int32, (n, n), 1)
        return jnp.where(r == q, jnp.where(keep, DAMPING, 1.0), 0.0)

    p_kept = kept(p)
    from_sibling(0)
    hp0 = jnp.where(p_kept[:, :128], pcb[:, :, 0].reshape(512, 128), 0.0).astype(BF16)
    t_ref[:128, :128] = dot(jnp.transpose(hp0), hp0) * scale + damping(p_kept[:, :128])

    def factor_block(b, _):
        s0 = pl.multiple_of(128 * b, 128)
        at = pl.ds(s0, 128)
        m, u = eliminate(t_ref[at, at], WIDTH)

        @pl.when(b == 0)
        def _():
            to_sibling(1)
            from_sibling(1)
            hp = jnp.concatenate([pcb[:, :, q].reshape(512, 128) for q in range(4)], 1)
            hp = jnp.where(p_kept, hp, 0.0).astype(BF16)
            hp_ref[...] = hp
            hpt = jnp.transpose(hp)
            hpt_ref[...] = hpt
            t_ref[...] = dot(hpt, hp) * scale + damping(p_kept)
            to_sibling(2)
            rows_over_x()

        @pl.when(b == 1)
        def _():
            columns_over_z()

        @pl.when(b == 2)
        def _():
            rows_over_cores()

        lane_block = lane // 128
        s = dot3(m, t_ref[at, :])
        m_ref[at, :] = jnp.where(lane_block < b, s, 0.0)
        u_ref[at, :] = jnp.where(lane_block > b, s, 0.0)
        m_ref[at, at] = m
        u_ref[at, at] = u
        s_ref[...] = s
        s_ref[:, at] = m

        for k in range(3):

            @pl.when(b == k)
            def _():
                under = slice(128 * k + 128, 512)
                parts = split(s_ref[...])
                left = tuple(jnp.transpose(v[:, under]) for v in parts)
                update = dot3(left, parts)
                t_ref[under, under] -= update[:, under]
                t_ref[under, : 128 * k + 128] = (
                    jnp.where(lane[:, : 128 * k + 128] < 128 * k, t_ref[under, : 128 * k + 128], 0.0)
                    - update[:, : 128 * k + 128]
                )

        return 0

    lax.fori_loop(0, 4, factor_block, 0)

    from_sibling(2)
    hp = hp_ref[...]
    hpr = jnp.concatenate([pcb[:, :, 4 + q].reshape(512, 128) for q in range(2)], 1)
    hpt = hpt_ref[...]
    drain(colb.at[:, :, 1 - z], r_col.at[1])
    hc = jnp.where(kept(j), colb[...].reshape(512, 512), 0.0).astype(BF16)
    hct = jnp.transpose(hc)
    below = (j > p).astype(F32)
    inside = (j == p).astype(F32)
    kc = dot(hct, hp) * (scale * below)
    cross_c = (dot(hct, hpr) * scale).astype(BF16)
    cross_p = (dot(hpt, hpr) * scale).astype(BF16)
    m_parts = split(m_ref[...])
    r = lax.broadcasted_iota(jnp.int32, (128, 128), 0)
    q = lax.broadcasted_iota(jnp.int32, (128, 128), 1)
    t_ref[...] = dot3(kc, m_parts, 1, 1)
    for k in range(4):
        at = slice(128 * k, 128 * k + 128)
        t_ref[at, at] -= jnp.where(r == q, inside, 0.0)
    gh, gl = split(dot3(t_ref[...], m_parts))
    outside = 1.0 - inside
    rest = hc.astype(F32) * outside - (dot(hp, gh, 1, 1) + dot(hp, gl, 1, 1))
    rh, rlow = split(rest)
    ch, cl = split(cross_c.astype(F32) * outside - (dot(gh, cross_p) + dot(gl, cross_p)))
    drain(pd.at[:, pl.ds(0, 7)], r_d.at[2])
    chosen_down = pd[...].reshape(256, 512)
    cout[...] = dot(ch, chosen_down) + dot(cl, chosen_down)
    drain(rowb.at[1 - c], r_row.at[3])
    lower = jnp.transpose(u_ref[...])
    for h in range(2):
        row = 2 * i + h
        r_kept = kept(row)
        hr = jnp.concatenate(
            [
                jnp.concatenate(
                    [rowb[ic, cc, 2 * h + t].reshape(128, 128) for t in range(2) for ic in range(2)], 0
                )
                for cc in range(4)
            ],
            1,
        )
        hrt = jnp.transpose(jnp.where(r_kept, hr, 0.0).astype(BF16))
        under = row > p
        high = jnp.where(under, rh, hc)
        low = jnp.where(under, rlow, jnp.zeros_like(rlow))
        out = (dot(hrt, high) + dot(hrt, low)) * scale
        rows = slice(512 * h, 512 * h + 512)
        fout[rows, :] = jnp.where((row == p) & (j == p), lower, out)
        on_diagonal = ((row == j) & (row != p)).astype(F32)
        for k in range(4):
            at = slice(128 * k, 128 * k + 128)
            rows = slice(512 * h + 128 * k, 512 * h + 128 * k + 128)
            fout[rows, at] += damping(r_kept[:, at]) * on_diagonal

    drain(tok.at[:, pl.ds(0, 15 * 256)], s_tok)
    drain(feat.at[c], s_sib)
    for n, (way, h, hops) in enumerate(CHAINS):
        for s in range(hops - 1):
            drain(sb.at[n, s], s_ch.at[n, s])
        drain(rl.at[n], s_last.at[n])
    drain(zr, s_z)
    drain(xb.at[pl.ds(0, 7)], s_x)
    drain(zb.at[pl.ds(0, 3)], s_zh.at[0])
    drain(zb2.at[pl.ds(0, 3)], s_zh.at[1])
    for n in range(3):
        drain(pcb.at[c, pl.ds(0, 15), panel_part(n)], s_p.at[n])
        drain(pcb.at[c, :, panel_part(n)], s_ps.at[n])
    self_row = (j // 2 == i) & ((j // 2) // 8 == c) & (i // 8 == c)

    @pl.when(self_row)
    def _():
        drain(hpc.at[pl.ds(0, 7)], s_row.at[0])

    @pl.when(jnp.logical_not(self_row))
    def _():
        drain(hpc, s_row.at[0])

    drain(rowb.at[c, x, pl.ds(0, 3)], s_row.at[1])
    drain(rowb.at[c, pl.ds(0, 3)], s_row.at[2])
    drain(part2, s_row.at[3])
    drain(colb.at[:, pl.ds(0, 7), z], s_col.at[0])
    drain(colb.at[:, :, z], s_col.at[1])
    drain(dxr.at[pl.ds(0, 7)], s_d.at[0])
    drain(dzr.at[pl.ds(0, 3)], s_d.at[1])
    drain(pd.at[:, pl.ds(0, 7)], s_d.at[2])


def local(tokens, gate_weight, up_weight, down_weight, pruned_blocks, panel_number):
    vmem = pl.BlockSpec(memory_space=pltpu.VMEM)
    smem = pl.BlockSpec(memory_space=pltpu.SMEM)
    hbm = pl.BlockSpec(memory_space=pl.ANY)
    dma = pltpu.SemaphoreType.DMA

    def b16(*shape):
        return pltpu.VMEM(shape, BF16)

    def f32(*shape):
        return pltpu.VMEM(shape, F32)

    return pl.pallas_call(
        body,
        out_shape=(pltpu.VMEM((1024, 512), F32), pltpu.VMEM((512, 512), F32)),
        in_specs=[hbm] * 4 + [smem] * 2,
        out_specs=(vmem, vmem),
        scratch_shapes=[
            b16(32, 8192), b16(512, 512), b16(512, 512), b16(512, 512),
            b16(2, 8, 64, 256), f32(8, 64, 1024),
            b16(8, 3, 64, 256), f32(8, 64, 256), b16(8, 3, 64, 256), f32(8, 2, 32, 256),
            b16(32, 1024), b16(32, 1024),
            b16(2, 16, 512), b16(8, 16, 128),
            b16(8, 16, 512),
            b16(4, 16, 128), b16(2, 16, 128), b16(4, 4, 16, 128), b16(4, 2, 16, 128),
            b16(2, 16, 6, 16, 128),
            b16(2, 8, 2, 16, 512), b16(2, 4, 4, 8, 16, 128),
            b16(8, 2, 16, 512), b16(8, 2, 16, 512), b16(2, 16, 512), b16(4, 2, 16, 512), b16(2, 8, 16, 512),
            f32(512, 512), f32(128, 512), f32(512, 512), f32(512, 512),
            b16(512, 512), b16(512, 512),
            dma((4,)), pltpu.SemaphoreType.REGULAR,
            dma, dma((5,)), dma, dma((5,)), dma((8, 3)), dma((8, 3)), dma((8,)), dma((8,)), dma, dma,
            dma, dma, dma((2,)), dma((2,)), dma((3,)), dma((3,)), dma((3,)), dma((3,)),
            dma((4,)), dma((4,)), dma((2,)), dma((2,)), dma((3,)), dma((3,)),
        ],
        compiler_params=pltpu.CompilerParams(
            collective_id=0, has_side_effects=True, vmem_limit_bytes=60 << 20
        ),
        name="prune",
    )(tokens, gate_weight, up_weight, down_weight, pruned_blocks, panel_number)


def solution(mesh):
    in_specs = (P("dp", None), P("dp", "tensor"), P("dp", "tensor"), P("tensor", "dp"), P(), P())
    out_specs = (P("dp", "tensor"), P("tensor", "dp"))
    return jax.shard_map(local, mesh=mesh, in_specs=in_specs, out_specs=out_specs, check_vma=False)
```
